512 devices in a mesh: outer: 16 (over y, x), inner: 32 (over z, core).
Axes of the slice: x: 4, y: 4, z: 16, core: 2. Of those that a mesh axis runs over, the one named last changes fastest.
Arguments:
- query_states: bfloat16 [65536, 2048], P(('outer', 'inner')), may hold values from -400 to 400
- key_states: bfloat16 [65536, 2048], P(('outer', 'inner')), may hold values from -13 to 13
- value_states: bfloat16 [65536, 2048], P(('outer', 'inner')), may hold values from -27 to 27
Outputs:
- attention_out: bfloat16 [65536, 2048], P(('outer', 'inner'))
The draws below stay inside these ranges and needn't reach their ends.
All inputs are finite; a program needn't handle non-finite values.
Results may differ from the reference program's by a relative error of at most 0.0038.
Values may be sent and summed in bfloat16 or wider, within the bound.
A program may use at most 64 MiB of HBM per device.

```python
import math
import jax
import jax.numpy as jnp
from jax import lax

HEADS = 16
HEAD_DIM = 128
LEAF = 128
WIDTH = 2048
SEQ = 65536
N_INNER = 32


def layered(seed_key, columns):
    layers_count = min(SEQ.bit_length() - 1, 16) + 1
    running = jax.random.truncated_normal(jax.random.fold_in(seed_key, layers_count - 1), -3.0, 3.0, (SEQ >> layers_count - 1, columns), jnp.float32)
    for layer_index in range(layers_count - 2, -1, -1):
        fresh = jax.random.truncated_normal(jax.random.fold_in(seed_key, layer_index), -3.0, 3.0, (SEQ >> layer_index, columns), jnp.float32)
        running = jnp.repeat(running, 2, axis=0) + fresh
    return running / math.sqrt(layers_count)


def draw_query_states(key, part):
    drawn = 1.25 * layered(jax.random.fold_in(key, 1), WIDTH)
    return drawn.astype(jnp.bfloat16)


def draw_key_states(key, part):
    base_draw = layered(jax.random.fold_in(key, 2), WIDTH)
    return base_draw.astype(jnp.bfloat16)


def draw_value_states(key, part):
    base_draw = 2.0 * layered(jax.random.fold_in(key, 3), WIDTH)
    return base_draw.astype(jnp.bfloat16)


def setup_inputs(seed: int = 0) -> dict:
    streams_of = jax.random.split(jax.random.key(seed), 4)
    return {
        "query_states": draw_query_states(jax.random.fold_in(streams_of[3], 71), 0),
        "key_states": draw_key_states(jax.random.fold_in(streams_of[3], 71), 0),
        "value_states": draw_value_states(jax.random.fold_in(streams_of[3], 71), 0),
    }


def halve_rows(array):
    paired = array.astype(jnp.float32).reshape(array.shape[0] // 2, 2, array.shape[1])
    return lax.optimization_barrier(((paired[:, 0] + paired[:, 1]) * 0.5).astype(jnp.bfloat16))

def level_terms(query_rows, key_rows, value_rows):
    shaped_q = query_rows.astype(jnp.float32).reshape(query_rows.shape[0], HEADS, HEAD_DIM)
    shaped_k = key_rows.astype(jnp.float32).reshape(key_rows.shape[0], HEADS, HEAD_DIM)
    shaped_v = value_rows.astype(jnp.float32).reshape(value_rows.shape[0], HEADS, HEAD_DIM)
    scores = jnp.einsum('rhe,che->hrc', shaped_q, shaped_k, precision=lax.Precision.HIGHEST) / math.sqrt(HEAD_DIM)
    peak_scores = lax.optimization_barrier(jnp.max(scores, axis=2))
    weights = jnp.exp(scores - peak_scores[:, :, None])
    totals = lax.optimization_barrier(jnp.sum(weights, axis=2))
    rounded = lax.optimization_barrier(weights.astype(jnp.bfloat16)).astype(jnp.float32)
    weighted = jnp.einsum('hrc,che->hre', rounded, shaped_v, precision=lax.Precision.HIGHEST)
    return (peak_scores, totals, weighted)

def spread_rows(terms, factor):
    return tuple((jnp.repeat(member, factor, axis=1) for member in terms))

def combine(level_parts):
    highest = level_parts[0][0]
    for member in level_parts[1:]:
        highest = jnp.maximum(highest, member[0])
    numerator = jnp.zeros(level_parts[0][2].shape, jnp.float32)
    denominator = jnp.zeros(level_parts[0][1].shape, jnp.float32)
    for member in level_parts:
        factor = jnp.exp(member[0] - highest)
        numerator = numerator + factor[:, :, None] * member[2]
        denominator = denominator + factor * member[1]
    result = numerator / denominator[:, :, None]
    return jnp.transpose(result, (1, 0, 2)).reshape(result.shape[1], HEADS * HEAD_DIM).astype(jnp.bfloat16)

def reference(query_states, key_states, value_states):
    top_level = (2 * N_INNER).bit_length() - 1
    block_count = SEQ // LEAF
    pooled_keys = [key_states]
    pooled_values = [value_states]
    for level_index in range(top_level):
        pooled_keys.append(halve_rows(pooled_keys[-1]))
        pooled_values.append(halve_rows(pooled_values[-1]))

    def one_block(block_index):
        row_start = (block_index * LEAF).astype(jnp.int32)
        query_rows = lax.dynamic_slice_in_dim(query_states, row_start, LEAF, 0)
        pair_start = (block_index // 2 * (2 * LEAF)).astype(jnp.int32)
        near_keys = lax.dynamic_slice_in_dim(key_states, pair_start, 2 * LEAF, 0)
        near_values = lax.dynamic_slice_in_dim(value_states, pair_start, 2 * LEAF, 0)
        level_parts = [level_terms(query_rows, near_keys, near_values)]
        coarse = query_rows
        for level_index in range(1, top_level + 1):
            coarse = halve_rows(coarse)
            partner = ((jnp.right_shift(block_index, level_index) ^ 1) * LEAF).astype(jnp.int32)
            far_keys = lax.dynamic_slice_in_dim(pooled_keys[level_index], partner, LEAF, 0)
            far_values = lax.dynamic_slice_in_dim(pooled_values[level_index], partner, LEAF, 0)
            terms = level_terms(coarse, far_keys, far_values)
            level_parts.append(spread_rows(terms, 2 ** level_index))
        return combine(level_parts)
    outputs = lax.map(one_block, jnp.arange(block_count, dtype=jnp.int32))
    return outputs.reshape(SEQ, HEADS * HEAD_DIM)
```

```python
import math

import jax
import jax.numpy as jnp
from jax import lax
from jax.experimental import pallas as pl
from jax.experimental.pallas import tpu as pltpu
from jax.sharding import PartitionSpec as P

HEADS = 16
HALF = HEADS // 2
DIM = 128
LEAF = 128
CHIPS = 16
CHUNKS = 4
PER = HALF // CHUNKS
SCALE = 1.0 / math.sqrt(DIM)
SCALE2 = SCALE * math.log2(math.e)
MESH = pl.DeviceIdType.MESH
BF = jnp.bfloat16
F32 = jnp.float32


def nn(a, b):
    return lax.dot_general(a, b, (((1,), (0,)), ((), ())), preferred_element_type=F32)


def nt(a, b):
    return lax.dot_general(a, b, (((1,), (1,)), ((), ())), preferred_element_type=F32)


def grid_of(rows, columns):
    return (
        lax.broadcasted_iota(jnp.int32, (rows, columns), 0),
        lax.broadcasted_iota(jnp.int32, (rows, columns), 1),
    )


def halving(rows):
    i, j = grid_of(rows // 2, rows)
    return jnp.where((j >> 1) == i, 0.5, 0.0).astype(BF)


def halving_spread(rows, level):
    i, j = grid_of(rows, rows)
    first = (j & ((1 << (level - 1)) - 1)) == 0
    return jnp.where(((i >> level) == (j >> level)) & first, 0.5, 0.0).astype(BF)


def with_ones(values):
    return jnp.concatenate([values, jnp.ones_like(values)], axis=1)


def attend(scores, values):
    peak = jnp.max(scores[0], axis=1, keepdims=True)
    for s in scores[1:]:
        peak = jnp.maximum(peak, jnp.max(s, axis=1, keepdims=True))
    total = None
    for s, v in zip(scores, values):
        w = jnp.exp2((s - peak) * SCALE2).astype(BF)
        part = nn(w, with_ones(v))
        total = part if total is None else total + part
    den = total[:, DIM:]
    return total[:, :DIM] / den, peak, jnp.log(den)


def split3(x):
    high = x.astype(BF)
    rest = x - high.astype(F32)
    mid = rest.astype(BF)
    low = (rest - mid.astype(F32)).astype(BF)
    return jnp.concatenate([high, mid, low], axis=1)


def kernel(
    q_in, k_in, v_in, out,
    full, near, kv1_s, kv1_r, far_s, far_r, kv3, kv4_s, kv5_s, kv6_s, kv4_r, kv5_r, kv6_r,
    q_up, res_s, stat_s, res_r, stat_r, near_o, near_m, near_l, done,
    load_sem, own_sem, near_ss, near_rs, far_ss, far_rs, kv1_ss, kv1_rs, up_ss, up_rs,
    res_ss, res_rs, stat_ss, stat_rs, out_ls, out_ss, out_rs,
):
    o = lax.axis_index("outer")
    n = lax.axis_index("inner")
    c = n % 2
    z = n // 2
    half = z // 8
    zl = z % 8
    other = 1 - c
    differ = (half + c) % 2
    mate = (o, 2 * z + other)
    zs = z + 1 - 2 * (z % 2)
    o1 = o + 1 - 2 * (o % 2)
    o2 = o + 2 - 4 * ((o // 2) % 2)
    o3 = o2 + 1 - 2 * (o2 % 2)
    inputs = (q_in, k_in, v_in)

    def remote(src, dst, ss, rs, device):
        return pltpu.make_async_remote_copy(
            src_ref=src, dst_ref=dst, send_sem=ss, recv_sem=rs, device_id=device, device_id_type=MESH
        )

    loads = [pltpu.make_async_copy(inputs[i], full.at[i], load_sem.at[i]) for i in range(3)]
    for copy in loads:
        copy.start()

    barrier = pltpu.get_barrier_semaphore()

    def greet(i, carry):
        d = 16 * c + i

        @pl.when(d != n)
        def _():
            pl.semaphore_signal(barrier, inc=1, device_id=(o, d), device_id_type=MESH)

        return carry

    lax.fori_loop(0, 16, greet, 0)
    pl.semaphore_signal(barrier, inc=1, device_id=mate, device_id_type=MESH)
    for cc in range(2):
        for device in ((o, 2 * zs + cc), (o1, 2 * z + cc), (o2, 2 * z + cc), (o3, 2 * z + cc)):
            pl.semaphore_signal(barrier, inc=1, device_id=device, device_id_type=MESH)

    own = [
        pltpu.make_async_copy(
            inputs[i].at[:, pl.ds(1024 * c, 1024)], near.at[i, pl.ds(128 * c, 128), :], own_sem.at[i]
        )
        for i in range(3)
    ]
    for copy in own:
        copy.start()

    for copy in loads:
        copy.wait()

    half128 = halving(128)
    half64 = halving(64)

    def pool(i, carry):
        at = pl.ds(pl.multiple_of(i * 512, 512), 512)
        one = [nn(half128, full[a, :, at]).astype(BF) for a in range(3)]
        two = [nn(half64, x).astype(BF) for x in one]
        for u in range(4):
            h = i * 4 + u
            cut = slice(u * DIM, (u + 1) * DIM)
            kv1_s[h] = jnp.concatenate([one[1][:, cut], one[2][:, cut]], axis=1)
            far_s[h] = jnp.concatenate([two[0][:, cut], two[1][:, cut], two[2][:, cut]], axis=1)
        return carry

    lax.fori_loop(0, 4, pool, 0)

    pl.semaphore_wait(barrier, 24 + differ)

    mine = zl * 2 + c

    @pl.when(differ == 0)
    def _():
        pltpu.make_async_copy(far_s.at[z], far_r.at[mine], far_rs.at[mine]).start()

    @pl.when(differ == 1)
    def _():
        remote(far_s.at[z], far_r.at[mine], far_ss.at[0], far_rs.at[mine], mate).start()

    def far_copy(k):
        step = (k + 1) // 2
        zz = (z + 16 + step * (2 * (k % 2) - 1)) % 16
        return remote(far_s.at[zz], far_r.at[mine], far_ss.at[k], far_rs.at[mine], (o, 2 * zz + half))

    def send_far(k, carry):
        far_copy(k).start()
        return carry

    lax.fori_loop(1, 16, send_far, 0)

    near_copies = [
        remote(
            inputs[i].at[:, pl.ds(1024 * other, 1024)], near.at[i, pl.ds(128 * c, 128), :],
            near_ss.at[i], near_rs.at[i], mate,
        )
        for i in range(3)
    ]
    for copy in near_copies:
        copy.start()

    def wait_far(s, carry):
        remote(far_s.at[0], far_r.at[s], far_ss.at[0], far_rs.at[s], mate).wait_recv()
        return carry

    lax.fori_loop(0, 16, wait_far, 0)

    def kv1_copy(q, cc):
        return remote(
            kv1_s.at[pl.ds(HALF * cc + PER * q, PER)],
            kv1_r.at[pl.ds(PER * q, PER), pl.ds(64 * c, 64), :],
            kv1_ss.at[cc, q], kv1_rs.at[c, q], (o, 2 * zs + cc),
        )

    def send_kv1(q, carry):
        for cc in range(2):
            kv1_copy(q, cc).start()
        return carry

    lax.fori_loop(0, CHUNKS, send_kv1, 0)

    kv2 = [far_r[pl.ds(4 * g, 4), :, DIM:].reshape(128, 2 * DIM) for g in range(4)]
    for g in range(4):
        kv3[pl.ds(64 * g, 64), :] = nn(half128, kv2[g]).astype(BF)
    for g in range(2):
        kv4_s[pl.ds(64 * g, 64), :] = nn(half128, kv3[pl.ds(128 * g, 128), :]).astype(BF)
    up = [remote(kv4_s, kv4_r, up_ss.at[0], up_rs.at[0], mate)]
    up[0].start()
    kv5 = nn(half128, kv4_s[...]).astype(BF)
    kv5_s[...] = kv5
    for cc in range(2):
        copy = remote(kv5_s, kv5_r.at[c], up_ss.at[1 + cc], up_rs.at[1 + c], (o1, 2 * z + cc))
        copy.start()
        up.append(copy)
    kv6_s[...] = nn(half64, kv5).astype(BF)
    slot = 2 * (o % 2) + c
    for k, line in enumerate((o2, o3)):
        for cc in range(2):
            copy = remote(
                kv6_s, kv6_r.at[slot], up_ss.at[3 + 2 * k + cc], up_rs.at[3 + slot], (line, 2 * z + cc)
            )
            copy.start()
            up.append(copy)

    spreads = [halving_spread(128, level) for level in range(1, 5)]

    def pool_queries(g, carry):
        x = far_r[pl.ds(4 * g, 4), :, :DIM].reshape(128, DIM)
        for level in range(4):
            x = nn(spreads[level], x).astype(BF)
            q_up[level, g] = x
        return carry

    lax.fori_loop(0, 4, pool_queries, 0)

    remote(kv4_s, kv4_r, up_ss.at[0], up_rs.at[0], mate).wait_recv()
    for cc in range(2):
        remote(kv5_s, kv5_r.at[cc], up_ss.at[1], up_rs.at[1 + cc], mate).wait_recv()
    for s in range(4):
        remote(kv6_s, kv6_r.at[s], up_ss.at[3], up_rs.at[3 + s], mate).wait_recv()

    eye_i, eye_j = grid_of(128, 128)
    eye = eye_i == eye_j

    def result_copies(i):
        device = (o, 2 * (8 * c + i) + half)
        return (
            remote(res_s.at[i], res_r.at[zl], res_ss.at[i], res_rs.at[zl], device),
            remote(stat_s.at[i // 2], stat_r.at[zl], stat_ss.at[i], stat_rs.at[zl], device),
        )

    def is_self(i):
        return 8 * c + i + 16 * differ == z

    def far_attention(g, carry):
        q2 = far_r[pl.ds(4 * g, 4), :, :DIM].reshape(128, DIM)
        g1 = g + 1 - 2 * (g % 2)
        keys = [
            far_r[pl.ds(4 * g1, 4), :, DIM:].reshape(128, 2 * DIM),
            kv3[pl.ds(pl.multiple_of(128 * (1 - g // 2), 128), 128), :],
            kv4_r[...],
            kv5_r[...].reshape(128, 2 * DIM),
            kv6_r[...].reshape(128, 2 * DIM),
        ]
        queries = [q2] + [q_up[level, g] for level in range(4)]
        scores = [nt(q, kv[:, :DIM]) for q, kv in zip(queries, keys)]
        result, peak, total = attend(scores, [kv[:, DIM:] for kv in keys])
        res_s[2 * g] = result[:64].astype(BF)
        res_s[2 * g + 1] = result[64:].astype(BF)
        stat_s[g, 0:1, :] = jnp.sum(jnp.where(eye, peak, 0.0), axis=0, keepdims=True)
        stat_s[g, 1:2, :] = jnp.sum(jnp.where(eye, total, 0.0), axis=0, keepdims=True)
        for u in range(2):
            i = 2 * g + u

            @pl.when(is_self(i))
            def _():
                pltpu.make_async_copy(res_s.at[i], res_r.at[zl], res_rs.at[zl]).start()
                pltpu.make_async_copy(stat_s.at[g], stat_r.at[zl], stat_rs.at[zl]).start()

            @pl.when(jnp.logical_not(is_self(i)))
            def _():
                for copy in result_copies(i):
                    copy.start()

        return carry

    lax.fori_loop(0, 4, far_attention, 0)

    for copy in own:
        copy.wait()
    for i in range(3):
        remote(
            inputs[i].at[:, pl.ds(1024 * other, 1024)], near.at[i, pl.ds(128 * other, 128), :],
            near_ss.at[i], near_rs.at[i], mate,
        ).wait_recv()
    pairs = halving_spread(256, 1)

    def near_attention(q, carry):
        for cc in range(2):
            remote(
                kv1_s.at[pl.ds(0, PER)], kv1_r.at[pl.ds(PER * q, PER), pl.ds(64 * cc, 64), :],
                kv1_ss.at[0, q], kv1_rs.at[cc, q], mate,
            ).wait_recv()
        for u in range(PER):
            j = PER * q + u
            at = pl.ds(pl.multiple_of(j * DIM, DIM), DIM)
            x = near[0, :, at]
            x1 = nn(pairs, x).astype(BF)
            kv1 = kv1_r[j]
            scores = [nt(x, near[1, :, at]), nt(x1, kv1[:, :DIM])]
            result, peak, total = attend(scores, [near[2, :, at], kv1[:, DIM:]])
            near_o[j] = result
            near_m[j] = jnp.broadcast_to(peak, (256, DIM))
            near_l[j] = total
        return carry

    lax.fori_loop(0, CHUNKS, near_attention, 0)

    ri, rj = grid_of(256, 64)
    repeat4 = jnp.where((ri >> 2) == rj, 1.0, 0.0).astype(BF)
    si, sj = grid_of(256, DIM)
    pick = jnp.where((si >> 2) + 64 * (z % 2) == sj, 1.0, 0.0).astype(BF)
    pick3 = jnp.concatenate([pick, pick, pick], axis=1)

    def out_copies(j):
        at = pl.ds(pl.multiple_of((HALF * c + j) * DIM, DIM), DIM)
        return (
            pltpu.make_async_copy(done.at[j, pl.ds(128 * c, 128), :], out.at[:, at], out_ls.at[j]),
            remote(done.at[j, pl.ds(128 * other, 128), :], out.at[:, at], out_ss.at[j], out_rs.at[j], mate),
        )

    def merge(q, carry):
        for u in range(2):
            j = 2 * q + u
            remote(res_s.at[0], res_r.at[j], res_ss.at[0], res_rs.at[j], mate).wait_recv()
            remote(stat_s.at[0], stat_r.at[j], stat_ss.at[0], stat_rs.at[j], mate).wait_recv()
            coarse = nn(repeat4, res_r[j])
            peak = nt(pick3, jnp.broadcast_to(split3(stat_r[j, 0:1, :]), (DIM, 3 * DIM)))
            total = nt(pick3, jnp.broadcast_to(split3(stat_r[j, 1:2, :]), (DIM, 3 * DIM)))
            gap = (peak - near_m[j]) * SCALE + (total - near_l[j])
            share = 1.0 / (1.0 + jnp.exp(-gap))
            fine = near_o[j]
            done[j] = (fine + share * (coarse - fine)).astype(BF)
            for copy in out_copies(j):
                copy.start()
        return carry

    lax.fori_loop(0, HALF // 2, merge, 0)

    @pl.when(differ == 1)
    def _():
        remote(far_s.at[z], far_r.at[mine], far_ss.at[0], far_rs.at[mine], mate).wait_send()

    def end_far(k, carry):
        far_copy(k).wait_send()
        return carry

    lax.fori_loop(1, 16, end_far, 0)
    for copy in near_copies:
        copy.wait_send()

    def end_kv1(q, carry):
        for cc in range(2):
            kv1_copy(q, cc).wait_send()
        return carry

    lax.fori_loop(0, CHUNKS, end_kv1, 0)
    for copy in up:
        copy.wait_send()

    def end_results(i, carry):
        @pl.when(jnp.logical_not(is_self(i)))
        def _():
            for copy in result_copies(i):
                copy.wait_send()

        return carry

    lax.fori_loop(0, 8, end_results, 0)

    def end_out(j, carry):
        local, far = out_copies(j)
        local.wait()
        far.wait_send()
        at = pl.ds(pl.multiple_of((HALF * other + j) * DIM, DIM), DIM)
        remote(done.at[j, pl.ds(0, 128), :], out.at[:, at], out_ss.at[j], out_rs.at[j], mate).wait_recv()
        return carry

    lax.fori_loop(0, HALF, end_out, 0)


def body(query_states, key_states, value_states):
    dma = pltpu.SemaphoreType.DMA
    vmem = pltpu.VMEM
    return pl.pallas_call(
        kernel,
        out_shape=jax.ShapeDtypeStruct(query_states.shape, BF),
        in_specs=[pl.BlockSpec(memory_space=pl.ANY)] * 3,
        out_specs=pl.BlockSpec(memory_space=pl.ANY),
        scratch_shapes=[
            vmem((3, LEAF, HEADS * DIM), BF),
            vmem((3, 2 * LEAF, HALF * DIM), BF),
            vmem((HEADS, 64, 2 * DIM), BF),
            vmem((HALF, 128, 2 * DIM), BF),
            vmem((HEADS, 32, 3 * DIM), BF),
            vmem((CHIPS, 32, 3 * DIM), BF),
            vmem((256, 2 * DIM), BF),
            vmem((128, 2 * DIM), BF),
            vmem((64, 2 * DIM), BF),
            vmem((32, 2 * DIM), BF),
            vmem((128, 2 * DIM), BF),
            vmem((2, 64, 2 * DIM), BF),
            vmem((4, 32, 2 * DIM), BF),
            vmem((4, 4, 128, DIM), BF),
            vmem((8, 64, DIM), BF),
            vmem((4, 2, DIM), F32),
            vmem((8, 64, DIM), BF),
            vmem((8, 2, DIM), F32),
            vmem((HALF, 256, DIM), F32),
            vmem((HALF, 256, DIM), F32),
            vmem((HALF, 256, DIM), F32),
            vmem((HALF, 256, DIM), BF),
            dma((3,)), dma((3,)), dma((3,)), dma((3,)),
            dma((16,)), dma((16,)), dma((2, CHUNKS)), dma((2, CHUNKS)), dma((7,)), dma((7,)),
            dma((8,)), dma((8,)), dma((8,)), dma((8,)), dma((8,)), dma((8,)), dma((8,)),
        ],
        compiler_params=pltpu.CompilerParams(
            collective_id=0, has_side_effects=True, vmem_limit_bytes=32 * 1024 * 1024
        ),
        cost_estimate=pl.CostEstimate(flops=600_000_000, bytes_accessed=3_000_000, transcendentals=1_200_000),
        name="tree_attention",
    )(query_states, key_states, value_states)


def solution(mesh):
    placed = P(("outer", "inner"), None)
    return jax.shard_map(body, mesh=mesh, in_specs=(placed,) * 3, out_specs=placed, check_vma=False)
```

```python
import math

import jax
import jax.numpy as jnp
from jax import lax
from jax.experimental import pallas as pl
from jax.experimental.pallas import tpu as pltpu
from jax.sharding import PartitionSpec as P

HEADS = 16
HALF = HEADS // 2
DIM = 128
LEAF = 128
CHIPS = 16
CHUNKS = 4
PER = HALF // CHUNKS
SCALE = 1.0 / math.sqrt(DIM)
SCALE2 = SCALE * math.log2(math.e)
MESH = pl.DeviceIdType.MESH
BF = jnp.bfloat16
F32 = jnp.float32


def nn(a, b):
    return lax.dot_general(a, b, (((1,), (0,)), ((), ())), preferred_element_type=F32)


def nt(a, b):
    return lax.dot_general(a, b, (((1,), (1,)), ((), ())), preferred_element_type=F32)


def grid_of(rows, columns):
    return (
        lax.broadcasted_iota(jnp.int32, (rows, columns), 0),
        lax.broadcasted_iota(jnp.int32, (rows, columns), 1),
    )


def halving(rows):
    i, j = grid_of(rows // 2, rows)
    return jnp.where((j >> 1) == i, 0.5, 0.0).astype(BF)


def halving_spread(rows, level):
    i, j = grid_of(rows, rows)
    first = (j & ((1 << (level - 1)) - 1)) == 0
    return jnp.where(((i >> level) == (j >> level)) & first, 0.5, 0.0).astype(BF)


def with_ones(values):
    return jnp.concatenate([values, jnp.ones_like(values)], axis=1)


def attend(scores, values):
    peak = jnp.max(scores[0], axis=1, keepdims=True)
    for s in scores[1:]:
        peak = jnp.maximum(peak, jnp.max(s, axis=1, keepdims=True))
    total = None
    for s, v in zip(scores, values):
        w = jnp.exp2((s - peak) * SCALE2).astype(BF)
        part = nn(w, with_ones(v))
        total = part if total is None else total + part
    den = total[:, DIM:]
    return total[:, :DIM] / den, peak, jnp.log(den)


def split3(x):
    high = x.astype(BF)
    rest = x - high.astype(F32)
    mid = rest.astype(BF)
    low = (rest - mid.astype(F32)).astype(BF)
    return jnp.concatenate([high, mid, low], axis=1)


def as_rows(eye, peak, total):
    return jnp.concatenate(
        [
            jnp.sum(jnp.where(eye, peak, 0.0), axis=0, keepdims=True),
            jnp.sum(jnp.where(eye, total, 0.0), axis=0, keepdims=True),
        ],
        axis=0,
    )


def spread_stats(pick3, stats):
    parts = split3(stats)
    both = nt(
        pick3,
        jnp.concatenate(
            [jnp.broadcast_to(parts[0:1], (DIM, 3 * DIM)), jnp.broadcast_to(parts[1:2], (DIM, 3 * DIM))],
            axis=0,
        ),
    )
    return both[:, :DIM], both[:, DIM:]


def kernel(
    q_in, k_in, v_in, out,
    full, near, kv1_s, kv1_r, q2_s, q2_r, kv2_s, kv2_r, far_s, far_r,
    kv4_s, kv5_s, kv6_s, kv4_r, kv5_r, kv6_r, q_up,
    res2_s, stat2_s, res2_r, stat2_r, res_s, stat_s, res_r, stat_r, done,
    load_sem, own_sem, near_ss, near_rs, kv1_ss, kv1_rs, q2_ss, q2_rs, kv2_ss, kv2_rs, far_ss, far_rs,
    up_ss, up_rs, res2_ss, res2_rs, stat2_ss, stat2_rs, res_ss, res_rs, stat_ss, stat_rs,
    out_ls, out_ss, out_rs,
):
    o = lax.axis_index("outer")
    n = lax.axis_index("inner")
    c = n % 2
    z = n // 2
    half = z // 8
    zl = z % 8
    quad = z // 4
    zq = z % 4
    gq = zq // 2
    zp = z % 2
    other = 1 - c
    differ = (half + c) % 2
    mate = (o, 2 * z + other)
    zs = z + 1 - 2 * zp
    o1 = o + 1 - 2 * (o % 2)
    o2 = o + 2 - 4 * ((o // 2) % 2)
    o3 = o2 + 1 - 2 * (o2 % 2)
    inputs = (q_in, k_in, v_in)

    def remote(src, dst, ss, rs, device):
        return pltpu.make_async_remote_copy(
            src_ref=src, dst_ref=dst, send_sem=ss, recv_sem=rs, device_id=device, device_id_type=MESH
        )

    def start_either(here, src, dst, ss, rs, device):
        @pl.when(here)
        def _():
            pltpu.make_async_copy(src, dst, rs).start()

        @pl.when(jnp.logical_not(here))
        def _():
            remote(src, dst, ss, rs, device).start()

    def end_either(here, src, dst, ss, rs, device):
        @pl.when(jnp.logical_not(here))
        def _():
            remote(src, dst, ss, rs, device).wait_send()

    def load(i, part):
        at = pl.ds(512 * part, 512)
        return pltpu.make_async_copy(inputs[i].at[:, at], full.at[i, :, at], load_sem.at[part, i])

    for part in range(4):
        for i in range(3):
            load(i, part).start()

    barrier = pltpu.get_barrier_semaphore()

    def greet(d):
        @pl.when(d != n)
        def _():
            pl.semaphore_signal(barrier, inc=1, device_id=(o, d), device_id_type=MESH)

    def greet_line(i, carry):
        greet(16 * c + i)
        return carry

    def greet_quad(i, carry):
        greet(8 * quad + i)
        return carry

    lax.fori_loop(0, 16, greet_line, 0)
    lax.fori_loop(0, 8, greet_quad, 0)
    for line in (o1, o2, o3):
        for cc in range(2):
            pl.semaphore_signal(barrier, inc=1, device_id=(line, 2 * z + cc), device_id_type=MESH)

    own = [
        pltpu.make_async_copy(
            inputs[i].at[:, pl.ds(1024 * c, 1024)], near.at[i, pl.ds(128 * c, 128), :], own_sem.at[i]
        )
        for i in range(3)
    ]
    for copy in own:
        copy.start()

    half128 = halving(128)
    half64 = halving(64)
    half32 = halving(32)

    for part in range(4):
        for i in range(3):
            load(i, part).wait()
        one = [nn(half128, full[i, :, part * 512 : (part + 1) * 512]).astype(BF) for i in range(3)]
        two = [nn(half64, x).astype(BF) for x in one]
        three = [nn(half32, x).astype(BF) for x in two]
        for u in range(4):
            h = part * 4 + u
            cut = slice(u * DIM, (u + 1) * DIM)
            kv1_s[h] = jnp.concatenate([one[1][:, cut], one[2][:, cut]], axis=1)
            q2_s[h] = two[0][:, cut]
            kv2_s[h] = jnp.concatenate([two[1][:, cut], two[2][:, cut]], axis=1)
            far_s[h] = jnp.concatenate([x[:, cut] for x in three], axis=1)

    pl.semaphore_wait(barrier, 28 + differ)

    mine = zl * 2 + c

    def far_route(k):
        step = (k + 1) // 2
        zz = (z + 16 + step * (2 * (k % 2) - 1)) % 16
        here = zz + 16 * differ == z
        return here, far_s.at[zz], far_r.at[mine], far_ss.at[k], far_rs.at[mine], (o, 2 * zz + half)

    def send_far(k, carry):
        start_either(*far_route(15 - k))
        return carry

    lax.fori_loop(0, 16, send_far, 0)

    place = 2 * zp + c

    def level2_routes(i):
        k = (zq + i) % 4
        chip = 4 * quad + k
        rows = pl.ds(32 * place, 32)
        heads = pl.ds(4 * k, 4)
        away = (k + 4 - zq) % 4
        return (
            (
                away + (gq + c) % 2 == 0,
                q2_s.at[heads], q2_r.at[:, rows, :], q2_ss.at[i], q2_rs.at[place], (o, 2 * chip + gq),
            ),
            (
                away + (gq + other) % 2 == 0,
                kv2_s.at[heads], kv2_r.at[:, rows, :], kv2_ss.at[i], kv2_rs.at[place], (o, 2 * chip + 1 - gq),
            ),
        )

    def send_level2(i, carry):
        for route in level2_routes(3 - i):
            start_either(*route)
        return carry

    lax.fori_loop(0, 4, send_level2, 0)

    near_copies = [
        remote(
            inputs[i].at[:, pl.ds(1024 * other, 1024)], near.at[i, pl.ds(128 * c, 128), :],
            near_ss.at[i], near_rs.at[i], mate,
        )
        for i in range(3)
    ]
    for copy in near_copies:
        copy.start()

    def kv1_copy(q, cc):
        return remote(
            kv1_s.at[pl.ds(HALF * cc + PER * q, PER)],
            kv1_r.at[pl.ds(PER * q, PER), pl.ds(64 * c, 64), :],
            kv1_ss.at[cc, q], kv1_rs.at[c, q], (o, 2 * zs + cc),
        )

    def send_kv1(q, carry):
        for cc in range(2):
            kv1_copy(q, cc).start()
        return carry

    lax.fori_loop(0, CHUNKS, send_kv1, 0)

    def wait_far(s, carry):
        remote(far_s.at[0], far_r.at[s], far_ss.at[0], far_rs.at[s], mate).wait_recv()
        return carry

    lax.fori_loop(0, 16, wait_far, 0)

    for g in range(2):
        kv3 = far_r[pl.ds(8 * g, 8), :, DIM:].reshape(128, 2 * DIM)
        kv4_s[pl.ds(64 * g, 64), :] = nn(half128, kv3).astype(BF)
    kv4_copy = remote(kv4_s, kv4_r, up_ss.at[0], up_rs.at[0], mate)
    kv4_copy.start()
    up = [kv4_copy]
    kv5 = nn(half128, kv4_s[...]).astype(BF)
    kv5_s[...] = kv5
    for cc in range(2):
        copy = remote(kv5_s, kv5_r.at[c], up_ss.at[1 + cc], up_rs.at[1 + c], (o1, 2 * z + cc))
        copy.start()
        up.append(copy)
    kv6_s[...] = nn(half64, kv5).astype(BF)
    slot = 2 * (o % 2) + c
    for k, line in enumerate((o2, o3)):
        for cc in range(2):
            copy = remote(
                kv6_s, kv6_r.at[slot], up_ss.at[3 + 2 * k + cc], up_rs.at[3 + slot], (line, 2 * z + cc)
            )
            copy.start()
            up.append(copy)

    spreads = [halving_spread(128, level) for level in range(1, 4)]
    for g in range(2):
        x = far_r[pl.ds(8 * g, 8), :, :DIM].reshape(128, DIM)
        for level in range(3):
            x = nn(spreads[level], x).astype(BF)
            q_up[level, g] = x

    eye_i, eye_j = grid_of(128, 128)
    eye = eye_i == eye_j

    for s in range(4):
        rows = pl.ds(32 * s, 32)
        remote(q2_s.at[pl.ds(0, 4)], q2_r.at[:, rows, :], q2_ss.at[0], q2_rs.at[s], mate).wait_recv()
        remote(kv2_s.at[pl.ds(0, 4)], kv2_r.at[:, rows, :], kv2_ss.at[0], kv2_rs.at[s], mate).wait_recv()
    for u in range(4):
        kv2 = kv2_r[u]
        result, peak, total = attend([nt(q2_r[u], kv2[:, :DIM])], [kv2[:, DIM:]])
        for i in range(2):
            res2_s[i, u] = result[64 * i : 64 * i + 64].astype(BF)
        stat2_s[u] = as_rows(eye, peak, total)

    def level2_results(i):
        k = 2 * c + i
        device = (o, 2 * (4 * quad + k) + gq)
        here = (k + 4 - zq) % 4 + (gq + c) % 2 == 0
        heads = pl.ds(4 * zp, 4)
        return (
            (here, res2_s.at[i], res2_r.at[heads], res2_ss.at[i], res2_rs.at[zp], device),
            (here, stat2_s, stat2_r.at[heads], stat2_ss.at[i], stat2_rs.at[zp], device),
        )

    for i in range(2):
        for route in level2_results(i):
            start_either(*route)

    kv4_copy.wait_recv()
    for cc in range(2):
        remote(kv5_s, kv5_r.at[cc], up_ss.at[1], up_rs.at[1 + cc], mate).wait_recv()
    for s in range(4):
        remote(kv6_s, kv6_r.at[s], up_ss.at[3], up_rs.at[3 + s], mate).wait_recv()

    def results(i):
        device = (o, 2 * (8 * c + i) + half)
        here = 8 * c + i + 16 * differ == z
        return (
            (here, res_s.at[i], res_r.at[zl], res_ss.at[i], res_rs.at[zl], device),
            (here, stat_s.at[i // 4], stat_r.at[zl], stat_ss.at[i], stat_rs.at[zl], device),
        )

    for g in range(2):
        keys = [
            far_r[pl.ds(8 * (1 - g), 8), :, DIM:].reshape(128, 2 * DIM),
            kv4_r[...],
            kv5_r[...].reshape(128, 2 * DIM),
            kv6_r[...].reshape(128, 2 * DIM),
        ]
        queries = [far_r[pl.ds(8 * g, 8), :, :DIM].reshape(128, DIM)] + [q_up[level, g] for level in range(3)]
        scores = [nt(q, kv[:, :DIM]) for q, kv in zip(queries, keys)]
        result, peak, total = attend(scores, [kv[:, DIM:] for kv in keys])
        for i in range(4):
            res_s[4 * g + i] = result[32 * i : 32 * i + 32].astype(BF)
        stat_s[g] = as_rows(eye, peak, total)
        for i in range(4 * g, 4 * g + 4):
            for route in results(i):
                start_either(*route)

    for copy in own:
        copy.wait()
    for i in range(3):
        remote(
            inputs[i].at[:, pl.ds(1024 * other, 1024)], near.at[i, pl.ds(128 * other, 128), :],
            near_ss.at[i], near_rs.at[i], mate,
        ).wait_recv()
    pairs = halving_spread(256, 1)

    def repeat_of(level):
        i, j = grid_of(256, 256 >> level)
        return jnp.where((i >> level) == j, 1.0, 0.0).astype(BF)

    def pick_of(level, first):
        i, j = grid_of(256, DIM)
        pick = jnp.where((i >> level) + first == j, 1.0, 0.0).astype(BF)
        return jnp.concatenate([pick, pick, pick], axis=1)

    repeat2, repeat3 = repeat_of(2), repeat_of(3)
    pick2, pick3 = pick_of(2, 64 * zp), pick_of(3, 32 * zq)

    def out_copies(j):
        at = pl.ds(pl.multiple_of((HALF * c + j) * DIM, DIM), DIM)
        return (
            pltpu.make_async_copy(done.at[j, pl.ds(128 * c, 128), :], out.at[:, at], out_ls.at[j]),
            remote(done.at[j, pl.ds(128 * other, 128), :], out.at[:, at], out_ss.at[j], out_rs.at[j], mate),
        )

    def near_step(q, carry):
        for cc in range(2):
            remote(
                kv1_s.at[pl.ds(0, PER)], kv1_r.at[pl.ds(PER * q, PER), pl.ds(64 * cc, 64), :],
                kv1_ss.at[0, q], kv1_rs.at[cc, q], mate,
            ).wait_recv()

        @pl.when(q % (CHUNKS // 2) == 0)
        def _():
            p = q // (CHUNKS // 2)
            heads = pl.ds(4 * p, 4)
            remote(res2_s.at[0], res2_r.at[heads], res2_ss.at[0], res2_rs.at[p], mate).wait_recv()
            remote(stat2_s, stat2_r.at[heads], stat2_ss.at[0], stat2_rs.at[p], mate).wait_recv()

        for u in range(PER):
            j = PER * q + u
            remote(res_s.at[0], res_r.at[j], res_ss.at[0], res_rs.at[j], mate).wait_recv()
            remote(stat_s.at[0], stat_r.at[j], stat_ss.at[0], stat_rs.at[j], mate).wait_recv()
        for u in range(PER):
            j = PER * q + u
            at = pl.ds(pl.multiple_of(j * DIM, DIM), DIM)
            x = near[0, :, at]
            x1 = nn(pairs, x).astype(BF)
            kv1 = kv1_r[j]
            scores = [nt(x, near[1, :, at]), nt(x1, kv1[:, :DIM])]
            fine, peak, total = attend(scores, [near[2, :, at], kv1[:, DIM:]])
            peak2, total2 = spread_stats(pick2, stat2_r[j])
            peak3, total3 = spread_stats(pick3, stat_r[j])
            gap2 = (peak2 - peak) * SCALE + (total2 - total)
            gap3 = (peak3 - peak) * SCALE + (total3 - total)
            top = jnp.maximum(jnp.maximum(gap2, gap3), 0.0)
            w1, w2, w3 = jnp.exp(-top), jnp.exp(gap2 - top), jnp.exp(gap3 - top)
            merged = w1 * fine + w2 * nn(repeat2, res2_r[j]) + w3 * nn(repeat3, res_r[j])
            done[j] = (merged / (w1 + w2 + w3)).astype(BF)
            for copy in out_copies(j):
                copy.start()
        return carry

    lax.fori_loop(0, CHUNKS, near_step, 0)

    def end_far(k, carry):
        end_either(*far_route(k))
        return carry

    lax.fori_loop(0, 16, end_far, 0)

    def end_level2(i, carry):
        for route in level2_routes(i):
            end_either(*route)
        return carry

    lax.fori_loop(0, 4, end_level2, 0)
    for copy in near_copies:
        copy.wait_send()

    def end_kv1(q, carry):
        for cc in range(2):
            kv1_copy(q, cc).wait_send()
        return carry

    lax.fori_loop(0, CHUNKS, end_kv1, 0)
    for copy in up:
        copy.wait_send()
    for i in range(2):
        for route in level2_results(i):
            end_either(*route)

    def end_results(i, carry):
        for route in results(i):
            end_either(*route)
        return carry

    lax.fori_loop(0, 8, end_results, 0)

    def end_out(j, carry):
        local, far = out_copies(j)
        local.wait()
        far.wait_send()
        at = pl.ds(pl.multiple_of((HALF * other + j) * DIM, DIM), DIM)
        remote(done.at[j, pl.ds(0, 128), :], out.at[:, at], out_ss.at[j], out_rs.at[j], mate).wait_recv()
        return carry

    lax.fori_loop(0, HALF, end_out, 0)


def body(query_states, key_states, value_states):
    dma = pltpu.SemaphoreType.DMA
    vmem = pltpu.VMEM
    return pl.pallas_call(
        kernel,
        out_shape=jax.ShapeDtypeStruct(query_states.shape, BF),
        in_specs=[pl.BlockSpec(memory_space=pl.ANY)] * 3,
        out_specs=pl.BlockSpec(memory_space=pl.ANY),
        scratch_shapes=[
            vmem((3, LEAF, HEADS * DIM), BF),
            vmem((3, 2 * LEAF, HALF * DIM), BF),
            vmem((HEADS, 64, 2 * DIM), BF),
            vmem((HALF, 128, 2 * DIM), BF),
            vmem((HEADS, 32, DIM), BF),
            vmem((4, 128, DIM), BF),
            vmem((HEADS, 32, 2 * DIM), BF),
            vmem((4, 128, 2 * DIM), BF),
            vmem((HEADS, 16, 3 * DIM), BF),
            vmem((CHIPS, 16, 3 * DIM), BF),
            vmem((128, 2 * DIM), BF),
            vmem((64, 2 * DIM), BF),
            vmem((32, 2 * DIM), BF),
            vmem((128, 2 * DIM), BF),
            vmem((2, 64, 2 * DIM), BF),
            vmem((4, 32, 2 * DIM), BF),
            vmem((3, 2, 128, DIM), BF),
            vmem((2, 4, 64, DIM), BF),
            vmem((4, 2, DIM), F32),
            vmem((8, 64, DIM), BF),
            vmem((8, 2, DIM), F32),
            vmem((8, 32, DIM), BF),
            vmem((2, 2, DIM), F32),
            vmem((8, 32, DIM), BF),
            vmem((8, 2, DIM), F32),
            vmem((HALF, 256, DIM), BF),
            dma((4, 3)), dma((3,)), dma((3,)), dma((3,)), dma((2, CHUNKS)), dma((2, CHUNKS)),
            dma((4,)), dma((4,)), dma((4,)), dma((4,)), dma((16,)), dma((16,)),
            dma((7,)), dma((7,)), dma((2,)), dma((2,)), dma((2,)), dma((2,)),
            dma((8,)), dma((8,)), dma((8,)), dma((8,)),
            dma((8,)), dma((8,)), dma((8,)),
        ],
        compiler_params=pltpu.CompilerParams(
            collective_id=0, has_side_effects=True, vmem_limit_bytes=60 * 1024 * 1024
        ),
        cost_estimate=pl.CostEstimate(flops=600_000_000, bytes_accessed=3_000_000, transcendentals=1_200_000),
        name="tree_attention",
    )(query_states, key_states, value_states)


def solution(mesh):
    placed = P(("outer", "inner"), None)
    return jax.shard_map(body, mesh=mesh, in_specs=(placed,) * 3, out_specs=placed, check_vma=False)
```

```python
import math

import jax
import jax.numpy as jnp
from jax import lax
from jax.experimental import pallas as pl
from jax.experimental.pallas import tpu as pltpu
from jax.sharding import PartitionSpec as P

HEADS = 16
HALF = HEADS // 2
DIM = 128
LEAF = 128
CHIPS = 16
CHUNKS = 4
PER = HALF // CHUNKS
SCALE = 1.0 / math.sqrt(DIM)
SCALE2 = SCALE * math.log2(math.e)
MESH = pl.DeviceIdType.MESH
BF = jnp.bfloat16
F32 = jnp.float32


def nn(a, b):
    return lax.dot_general(a, b, (((1,), (0,)), ((), ())), preferred_element_type=F32)


def nt(a, b):
    return lax.dot_general(a, b, (((1,), (1,)), ((), ())), preferred_element_type=F32)


def grid_of(rows, columns):
    return (
        lax.broadcasted_iota(jnp.int32, (rows, columns), 0),
        lax.broadcasted_iota(jnp.int32, (rows, columns), 1),
    )


def halving(rows):
    i, j = grid_of(rows // 2, rows)
    return jnp.where((j >> 1) == i, 0.5, 0.0).astype(BF)


def halving_spread(rows, level):
    i, j = grid_of(rows, rows)
    first = (j & ((1 << (level - 1)) - 1)) == 0
    return jnp.where(((i >> level) == (j >> level)) & first, 0.5, 0.0).astype(BF)


def with_ones(values):
    return jnp.concatenate([values, jnp.ones_like(values)], axis=1)


def attend(scores, values):
    peak = jnp.max(scores[0], axis=1, keepdims=True)
    for s in scores[1:]:
        peak = jnp.maximum(peak, jnp.max(s, axis=1, keepdims=True))
    total = None
    for s, v in zip(scores, values):
        w = jnp.exp2((s - peak) * SCALE2).astype(BF)
        part = nn(w, with_ones(v))
        total = part if total is None else total + part
    den = total[:, DIM:]
    return total[:, :DIM] / den, peak, jnp.log(den)


def split3(x):
    high = x.astype(BF)
    rest = x - high.astype(F32)
    mid = rest.astype(BF)
    low = (rest - mid.astype(F32)).astype(BF)
    return jnp.concatenate([high, mid, low], axis=1)


def as_rows(eye, peak, total):
    return jnp.concatenate(
        [
            jnp.sum(jnp.where(eye, peak, 0.0), axis=0, keepdims=True),
            jnp.sum(jnp.where(eye, total, 0.0), axis=0, keepdims=True),
        ],
        axis=0,
    )


def spread_stats(pick3, stats):
    parts = split3(stats)
    both = nt(
        pick3,
        jnp.concatenate(
            [jnp.broadcast_to(parts[0:1], (DIM, 3 * DIM)), jnp.broadcast_to(parts[1:2], (DIM, 3 * DIM))],
            axis=0,
        ),
    )
    return both[:, :DIM], both[:, DIM:]


def kernel(
    q_in, k_in, v_in, out,
    full, near, kv1_s, kv1_r, q2_s, q2_r, kv2_s, kv2_r, far_s, far_r,
    kv4_s, kv5_s, kv6_s, kv4_r, kv5_r, kv6_r, q_up, near_o, near_m,
    res2_s, stat2_s, res2_r, stat2_r, res_s, stat_s, res_r, stat_r, done,
    load_sem, own_sem, near_ss, near_rs, kv1_ss, kv1_rs, q2_ss, q2_rs, kv2_ss, kv2_rs, far_ss, far_rs,
    up_ss, up_rs, res2_ss, res2_rs, stat2_ss, stat2_rs, res_ss, res_rs, stat_ss, stat_rs,
    out_ls, out_ss, out_rs,
):
    o = lax.axis_index("outer")
    n = lax.axis_index("inner")
    c = n % 2
    z = n // 2
    half = z // 8
    zl = z % 8
    quad = z // 4
    zq = z % 4
    gq = zq // 2
    zp = z % 2
    other = 1 - c
    differ = (half + c) % 2
    mate = (o, 2 * z + other)
    zs = z + 1 - 2 * zp
    o1 = o + 1 - 2 * (o % 2)
    o2 = o + 2 - 4 * ((o // 2) % 2)
    o3 = o2 + 1 - 2 * (o2 % 2)
    inputs = (q_in, k_in, v_in)

    def remote(src, dst, ss, rs, device):
        return pltpu.make_async_remote_copy(
            src_ref=src, dst_ref=dst, send_sem=ss, recv_sem=rs, device_id=device, device_id_type=MESH
        )

    def start_either(here, src, dst, ss, rs, device):
        @pl.when(here)
        def _():
            pltpu.make_async_copy(src, dst, rs).start()

        @pl.when(jnp.logical_not(here))
        def _():
            remote(src, dst, ss, rs, device).start()

    def end_either(here, src, dst, ss, rs, device):
        @pl.when(jnp.logical_not(here))
        def _():
            remote(src, dst, ss, rs, device).wait_send()

    quarters = [(quad + shift) % 4 for shift in (2, 1, 3, 0)]

    def load(i, step):
        at = pl.ds(pl.multiple_of(512 * quarters[step], 512), 512)
        return pltpu.make_async_copy(inputs[i].at[:, at], full.at[i, :, at], load_sem.at[step, i])

    for step in range(4):
        for i in range(3):
            load(i, step).start()

    barrier = pltpu.get_barrier_semaphore()

    def greet(d):
        @pl.when(d != n)
        def _():
            pl.semaphore_signal(barrier, inc=1, device_id=(o, d), device_id_type=MESH)

    def greet_line(i, carry):
        greet(16 * c + i)
        return carry

    def greet_quad(i, carry):
        greet(8 * quad + i)
        return carry

    lax.fori_loop(0, 16, greet_line, 0)
    lax.fori_loop(0, 8, greet_quad, 0)
    for line in (o1, o2, o3):
        for cc in range(2):
            pl.semaphore_signal(barrier, inc=1, device_id=(line, 2 * z + cc), device_id_type=MESH)

    own = [
        pltpu.make_async_copy(
            inputs[i].at[:, pl.ds(1024 * c, 1024)], near.at[i, pl.ds(128 * c, 128), :], own_sem.at[i]
        )
        for i in range(3)
    ]
    for copy in own:
        copy.start()

    half128 = halving(128)
    half64 = halving(64)
    half32 = halving(32)

    mine = zl * 2 + c

    def far_route(zz):
        here = zz + 16 * differ == z
        return here, far_s.at[zz], far_r.at[mine], far_ss.at[zz], far_rs.at[mine], (o, 2 * zz + half)

    place = 2 * zp + c

    def level2_routes(k):
        chip = 4 * quad + k
        rows = pl.ds(32 * place, 32)
        heads = pl.ds(4 * k, 4)
        away = (k + 4 - zq) % 4
        return (
            (
                away + (gq + c) % 2 == 0,
                q2_s.at[heads], q2_r.at[:, rows, :], q2_ss.at[k], q2_rs.at[place], (o, 2 * chip + gq),
            ),
            (
                away + (gq + other) % 2 == 0,
                kv2_s.at[heads], kv2_r.at[:, rows, :], kv2_ss.at[k], kv2_rs.at[place], (o, 2 * chip + 1 - gq),
            ),
        )

    for step in range(4):
        part = quarters[step]
        at = pl.ds(pl.multiple_of(512 * part, 512), 512)
        for i in range(3):
            load(i, step).wait()
        one = [nn(half128, full[i, :, at]).astype(BF) for i in range(3)]
        two = [nn(half64, x).astype(BF) for x in one]
        three = [nn(half32, x).astype(BF) for x in two]
        for u in range(4):
            h = part * 4 + u
            cut = slice(u * DIM, (u + 1) * DIM)
            far_s[h] = jnp.concatenate([x[:, cut] for x in three], axis=1)
            q2_s[h] = two[0][:, cut]
            kv2_s[h] = jnp.concatenate([two[1][:, cut], two[2][:, cut]], axis=1)
            kv1_s[h] = jnp.concatenate([one[1][:, cut], one[2][:, cut]], axis=1)
        if step == 0:
            pl.semaphore_wait(barrier, 28 + differ)

        def send_far(u, carry):
            start_either(*far_route(4 * part + u))
            return carry

        lax.fori_loop(0, 4, send_far, 0)
        for route in level2_routes(part):
            start_either(*route)

    near_copies = [
        remote(
            inputs[i].at[:, pl.ds(1024 * other, 1024)], near.at[i, pl.ds(128 * c, 128), :],
            near_ss.at[i], near_rs.at[i], mate,
        )
        for i in range(3)
    ]
    for copy in near_copies:
        copy.start()

    def kv1_copy(q, cc):
        return remote(
            kv1_s.at[pl.ds(HALF * cc + PER * q, PER)],
            kv1_r.at[pl.ds(PER * q, PER), pl.ds(64 * c, 64), :],
            kv1_ss.at[cc, q], kv1_rs.at[c, q], (o, 2 * zs + cc),
        )

    def send_kv1(q, carry):
        for cc in range(2):
            kv1_copy(q, cc).start()
        return carry

    lax.fori_loop(0, CHUNKS, send_kv1, 0)

    for copy in own:
        copy.wait()
    for i in range(3):
        remote(
            inputs[i].at[:, pl.ds(1024 * other, 1024)], near.at[i, pl.ds(128 * other, 128), :],
            near_ss.at[i], near_rs.at[i], mate,
        ).wait_recv()

    def level0(p, carry):
        for u in range(2):
            j = 2 * p + u
            at = pl.ds(pl.multiple_of(j * DIM, DIM), DIM)
            s = nt(near[0, :, at], near[1, :, at])
            peak = jnp.max(s, axis=1, keepdims=True)
            near_o[j] = nn(jnp.exp2((s - peak) * SCALE2).astype(BF), with_ones(near[2, :, at]))
            near_m[j] = jnp.broadcast_to(peak, (256, DIM))
        return carry

    lax.fori_loop(0, HALF // 2, level0, 0)

    def wait_far(s, carry):
        remote(far_s.at[0], far_r.at[s], far_ss.at[0], far_rs.at[s], mate).wait_recv()
        return carry

    lax.fori_loop(0, 16, wait_far, 0)

    for g in range(2):
        kv3 = far_r[pl.ds(8 * g, 8), :, DIM:].reshape(128, 2 * DIM)
        kv4_s[pl.ds(64 * g, 64), :] = nn(half128, kv3).astype(BF)
    kv4_copy = remote(kv4_s, kv4_r, up_ss.at[0], up_rs.at[0], mate)
    kv4_copy.start()
    up = [kv4_copy]
    kv5 = nn(half128, kv4_s[...]).astype(BF)
    kv5_s[...] = kv5
    for cc in range(2):
        copy = remote(kv5_s, kv5_r.at[c], up_ss.at[1 + cc], up_rs.at[1 + c], (o1, 2 * z + cc))
        copy.start()
        up.append(copy)
    kv6_s[...] = nn(half64, kv5).astype(BF)
    slot = 2 * (o % 2) + c
    for k, line in enumerate((o2, o3)):
        for cc in range(2):
            copy = remote(
                kv6_s, kv6_r.at[slot], up_ss.at[3 + 2 * k + cc], up_rs.at[3 + slot], (line, 2 * z + cc)
            )
            copy.start()
            up.append(copy)

    spreads = [halving_spread(128, level) for level in range(1, 4)]
    for g in range(2):
        x = far_r[pl.ds(8 * g, 8), :, :DIM].reshape(128, DIM)
        for level in range(3):
            x = nn(spreads[level], x).astype(BF)
            q_up[level, g] = x

    eye_i, eye_j = grid_of(128, 128)
    eye = eye_i == eye_j

    for s in range(4):
        rows = pl.ds(32 * s, 32)
        remote(q2_s.at[pl.ds(0, 4)], q2_r.at[:, rows, :], q2_ss.at[0], q2_rs.at[s], mate).wait_recv()
        remote(kv2_s.at[pl.ds(0, 4)], kv2_r.at[:, rows, :], kv2_ss.at[0], kv2_rs.at[s], mate).wait_recv()
    for u in range(4):
        kv2 = kv2_r[u]
        result, peak, total = attend([nt(q2_r[u], kv2[:, :DIM])], [kv2[:, DIM:]])
        for i in range(2):
            res2_s[i, u] = result[64 * i : 64 * i + 64].astype(BF)
        stat2_s[u] = as_rows(eye, peak, total)

    def level2_results(i):
        k = 2 * c + i
        device = (o, 2 * (4 * quad + k) + gq)
        here = (k + 4 - zq) % 4 + (gq + c) % 2 == 0
        heads = pl.ds(4 * zp, 4)
        return (
            (here, res2_s.at[i], res2_r.at[heads], res2_ss.at[i], res2_rs.at[zp], device),
            (here, stat2_s, stat2_r.at[heads], stat2_ss.at[i], stat2_rs.at[zp], device),
        )

    for i in range(2):
        for route in level2_results(i):
            start_either(*route)

    kv4_copy.wait_recv()
    for cc in range(2):
        remote(kv5_s, kv5_r.at[cc], up_ss.at[1], up_rs.at[1 + cc], mate).wait_recv()
    for s in range(4):
        remote(kv6_s, kv6_r.at[s], up_ss.at[3], up_rs.at[3 + s], mate).wait_recv()

    def results(i):
        device = (o, 2 * (8 * c + i) + half)
        here = 8 * c + i + 16 * differ == z
        return (
            (here, res_s.at[i], res_r.at[zl], res_ss.at[i], res_rs.at[zl], device),
            (here, stat_s.at[i // 4], stat_r.at[zl], stat_ss.at[i], stat_rs.at[zl], device),
        )

    for g in range(2):
        keys = [
            far_r[pl.ds(8 * (1 - g), 8), :, DIM:].reshape(128, 2 * DIM),
            kv4_r[...],
            kv5_r[...].reshape(128, 2 * DIM),
            kv6_r[...].reshape(128, 2 * DIM),
        ]
        queries = [far_r[pl.ds(8 * g, 8), :, :DIM].reshape(128, DIM)] + [q_up[level, g] for level in range(3)]
        scores = [nt(q, kv[:, :DIM]) for q, kv in zip(queries, keys)]
        result, peak, total = attend(scores, [kv[:, DIM:] for kv in keys])
        for i in range(4):
            res_s[4 * g + i] = result[32 * i : 32 * i + 32].astype(BF)
        stat_s[g] = as_rows(eye, peak, total)
        for i in range(4 * g, 4 * g + 4):
            for route in results(i):
                start_either(*route)

    pairs = halving_spread(256, 1)

    def level1(q, carry):
        for cc in range(2):
            remote(
                kv1_s.at[pl.ds(0, PER)], kv1_r.at[pl.ds(PER * q, PER), pl.ds(64 * cc, 64), :],
                kv1_ss.at[0, q], kv1_rs.at[cc, q], mate,
            ).wait_recv()
        for u in range(PER):
            j = PER * q + u
            at = pl.ds(pl.multiple_of(j * DIM, DIM), DIM)
            x1 = nn(pairs, near[0, :, at]).astype(BF)
            kv1 = kv1_r[j]
            s = nt(x1, kv1[:, :DIM])
            old = near_m[j]
            peak = jnp.maximum(old, jnp.max(s, axis=1, keepdims=True))
            kept = jnp.exp2((old - peak) * SCALE2)
            total = nn(jnp.exp2((s - peak) * SCALE2).astype(BF), with_ones(kv1[:, DIM:]))
            den = kept * near_o[j, :, DIM:] + total[:, DIM:]
            near_o[j, :, :DIM] = (kept * near_o[j, :, :DIM] + total[:, :DIM]) / den
            near_o[j, :, DIM:] = jnp.log(den)
            near_m[j] = peak
        return carry

    lax.fori_loop(0, CHUNKS, level1, 0)

    def repeat_of(level):
        i, j = grid_of(256, 256 >> level)
        return jnp.where((i >> level) == j, 1.0, 0.0).astype(BF)

    def pick_of(level, first):
        i, j = grid_of(256, DIM)
        pick = jnp.where((i >> level) + first == j, 1.0, 0.0).astype(BF)
        return jnp.concatenate([pick, pick, pick], axis=1)

    repeat2, repeat3 = repeat_of(2), repeat_of(3)
    pick2, pick3 = pick_of(2, 64 * zp), pick_of(3, 32 * zq)

    def merge2(p, carry):
        @pl.when(p % 2 == 0)
        def _():
            k = p // 2
            heads = pl.ds(4 * k, 4)
            remote(res2_s.at[0], res2_r.at[heads], res2_ss.at[0], res2_rs.at[k], mate).wait_recv()
            remote(stat2_s, stat2_r.at[heads], stat2_ss.at[0], stat2_rs.at[k], mate).wait_recv()

        for u in range(2):
            j = 2 * p + u
            fine, total, peak = near_o[j, :, :DIM], near_o[j, :, DIM:], near_m[j]
            coarse = nn(repeat2, res2_r[j])
            peak2, total2 = spread_stats(pick2, stat2_r[j])
            top = jnp.maximum(peak, peak2)
            w1 = jnp.exp((peak - top) * SCALE + total)
            w2 = jnp.exp((peak2 - top) * SCALE + total2)
            both = w1 + w2
            near_o[j, :, :DIM] = (w1 * fine + w2 * coarse) / both
            near_o[j, :, DIM:] = jnp.log(both)
            near_m[j] = top
        return carry

    lax.fori_loop(0, HALF // 2, merge2, 0)

    def out_copies(j):
        at = pl.ds(pl.multiple_of((HALF * c + j) * DIM, DIM), DIM)
        return (
            pltpu.make_async_copy(done.at[j, pl.ds(128 * c, 128), :], out.at[:, at], out_ls.at[j]),
            remote(done.at[j, pl.ds(128 * other, 128), :], out.at[:, at], out_ss.at[j], out_rs.at[j], mate),
        )

    def merge3(p, carry):
        for u in range(2):
            j = 2 * p + u
            remote(res_s.at[0], res_r.at[j], res_ss.at[0], res_rs.at[j], mate).wait_recv()
            remote(stat_s.at[0], stat_r.at[j], stat_ss.at[0], stat_rs.at[j], mate).wait_recv()
        for u in range(2):
            j = 2 * p + u
            fine, total, peak = near_o[j, :, :DIM], near_o[j, :, DIM:], near_m[j]
            coarse = nn(repeat3, res_r[j])
            peak3, total3 = spread_stats(pick3, stat_r[j])
            gap = (peak3 - peak) * SCALE + (total3 - total)
            share = 1.0 / (1.0 + jnp.exp(-gap))
            done[j] = (fine + share * (coarse - fine)).astype(BF)
            for copy in out_copies(j):
                copy.start()
        return carry

    lax.fori_loop(0, HALF // 2, merge3, 0)

    def end_far(k, carry):
        end_either(*far_route(k))
        return carry

    lax.fori_loop(0, 16, end_far, 0)

    def end_level2(i, carry):
        for route in level2_routes(i):
            end_either(*route)
        return carry

    lax.fori_loop(0, 4, end_level2, 0)
    for copy in near_copies:
        copy.wait_send()

    def end_kv1(q, carry):
        for cc in range(2):
            kv1_copy(q, cc).wait_send()
        return carry

    lax.fori_loop(0, CHUNKS, end_kv1, 0)
    for copy in up:
        copy.wait_send()
    for i in range(2):
        for route in level2_results(i):
            end_either(*route)

    def end_results(i, carry):
        for route in results(i):
            end_either(*route)
        return carry

    lax.fori_loop(0, 8, end_results, 0)

    def end_out(j, carry):
        local, far = out_copies(j)
        local.wait()
        far.wait_send()
        at = pl.ds(pl.multiple_of((HALF * other + j) * DIM, DIM), DIM)
        remote(done.at[j, pl.ds(0, 128), :], out.at[:, at], out_ss.at[j], out_rs.at[j], mate).wait_recv()
        return carry

    lax.fori_loop(0, HALF, end_out, 0)


def body(query_states, key_states, value_states):
    dma = pltpu.SemaphoreType.DMA
    vmem = pltpu.VMEM
    return pl.pallas_call(
        kernel,
        out_shape=jax.ShapeDtypeStruct(query_states.shape, BF),
        in_specs=[pl.BlockSpec(memory_space=pltpu.HBM)] * 3,
        out_specs=pl.BlockSpec(memory_space=pl.ANY),
        scratch_shapes=[
            vmem((3, LEAF, HEADS * DIM), BF),
            vmem((3, 2 * LEAF, HALF * DIM), BF),
            vmem((HEADS, 64, 2 * DIM), BF),
            vmem((HALF, 128, 2 * DIM), BF),
            vmem((HEADS, 32, DIM), BF),
            vmem((4, 128, DIM), BF),
            vmem((HEADS, 32, 2 * DIM), BF),
            vmem((4, 128, 2 * DIM), BF),
            vmem((HEADS, 16, 3 * DIM), BF),
            vmem((CHIPS, 16, 3 * DIM), BF),
            vmem((128, 2 * DIM), BF),
            vmem((64, 2 * DIM), BF),
            vmem((32, 2 * DIM), BF),
            vmem((128, 2 * DIM), BF),
            vmem((2, 64, 2 * DIM), BF),
            vmem((4, 32, 2 * DIM), BF),
            vmem((3, 2, 128, DIM), BF),
            vmem((HALF, 256, 2 * DIM), F32),
            vmem((HALF, 256, DIM), F32),
            vmem((2, 4, 64, DIM), BF),
            vmem((4, 2, DIM), F32),
            vmem((8, 64, DIM), BF),
            vmem((8, 2, DIM), F32),
            vmem((8, 32, DIM), BF),
            vmem((2, 2, DIM), F32),
            vmem((8, 32, DIM), BF),
            vmem((8, 2, DIM), F32),
            vmem((HALF, 256, DIM), BF),
            dma((4, 3)), dma((3,)), dma((3,)), dma((3,)), dma((2, CHUNKS)), dma((2, CHUNKS)),
            dma((4,)), dma((4,)), dma((4,)), dma((4,)), dma((16,)), dma((16,)),
            dma((7,)), dma((7,)), dma((2,)), dma((2,)), dma((2,)), dma((2,)),
            dma((8,)), dma((8,)), dma((8,)), dma((8,)),
            dma((8,)), dma((8,)), dma((8,)),
        ],
        compiler_params=pltpu.CompilerParams(
            collective_id=0, has_side_effects=True, vmem_limit_bytes=40 * 1024 * 1024
        ),
        cost_estimate=pl.CostEstimate(flops=600_000_000, bytes_accessed=3_000_000, transcendentals=1_200_000),
        name="tree_attention",
    )(*(pltpu.with_memory_space_constraint(x, pltpu.HBM) for x in (query_states, key_states, value_states)))


def solution(mesh):
    placed = P(("outer", "inner"), None)
    return jax.shard_map(body, mesh=mesh, in_specs=(placed,) * 3, out_specs=placed, check_vma=False)
```

```python
import math

import jax
import jax.numpy as jnp
from jax import lax
from jax.experimental import pallas as pl
from jax.experimental.pallas import tpu as pltpu
from jax.sharding import PartitionSpec as P

HEADS = 16
HALF = HEADS // 2
DIM = 128
LEAF = 128
CHIPS = 16
CHUNKS = 4
PER = HALF // CHUNKS
SCALE = 1.0 / math.sqrt(DIM)
SCALE2 = SCALE * math.log2(math.e)
MESH = pl.DeviceIdType.MESH
BF = jnp.bfloat16
F32 = jnp.float32


def nn(a, b):
    return lax.dot_general(a, b, (((1,), (0,)), ((), ())), preferred_element_type=F32)


def nt(a, b):
    return lax.dot_general(a, b, (((1,), (1,)), ((), ())), preferred_element_type=F32)


def grid_of(rows, columns):
    return (
        lax.broadcasted_iota(jnp.int32, (rows, columns), 0),
        lax.broadcasted_iota(jnp.int32, (rows, columns), 1),
    )


def halving(rows):
    i, j = grid_of(rows // 2, rows)
    return jnp.where((j >> 1) == i, 0.5, 0.0).astype(BF)


def halving_spread(rows, level):
    i, j = grid_of(rows, rows)
    first = (j & ((1 << (level - 1)) - 1)) == 0
    return jnp.where(((i >> level) == (j >> level)) & first, 0.5, 0.0).astype(BF)


def with_ones(values):
    return jnp.concatenate([values, jnp.ones_like(values)], axis=1)


def attend(scores, values):
    peak = jnp.max(scores[0], axis=1, keepdims=True)
    for s in scores[1:]:
        peak = jnp.maximum(peak, jnp.max(s, axis=1, keepdims=True))
    total = None
    for s, v in zip(scores, values):
        w = jnp.exp2((s - peak) * SCALE2).astype(BF)
        part = nn(w, with_ones(v))
        total = part if total is None else total + part
    den = total[:, DIM:]
    return total[:, :DIM] / den, peak, jnp.log(den)


def split3(x):
    high = x.astype(BF)
    rest = x - high.astype(F32)
    mid = rest.astype(BF)
    low = (rest - mid.astype(F32)).astype(BF)
    return jnp.concatenate([high, mid, low], axis=1)


def as_rows(eye, peak, total):
    return jnp.concatenate(
        [
            jnp.sum(jnp.where(eye, peak, 0.0), axis=0, keepdims=True),
            jnp.sum(jnp.where(eye, total, 0.0), axis=0, keepdims=True),
        ],
        axis=0,
    )


def spread_stats(pick3, stats):
    parts = split3(stats)
    both = nt(
        pick3,
        jnp.concatenate(
            [jnp.broadcast_to(parts[0:1], (DIM, 3 * DIM)), jnp.broadcast_to(parts[1:2], (DIM, 3 * DIM))],
            axis=0,
        ),
    )
    return both[:, :DIM], both[:, DIM:]


def kernel(
    q_in, k_in, v_in, out,
    full, near, kv1_s, kv1_r, q2_s, q2_r, kv2_s, kv2_r, far_s, far_r,
    kv4_s, kv5_s, kv6_s, kv4_r, kv5_r, kv6_r, q_up, near_o, near_m,
    res2_s, stat2_s, res2_r, stat2_r, res_s, stat_s, res_r, stat_r, done,
    load_sem, own_sem, near_ss, near_rs, kv1_ss, kv1_rs, q2_ss, q2_rs, kv2_ss, kv2_rs, far_ss, far_rs,
    up_ss, up_rs, res2_ss, res2_rs, stat2_ss, stat2_rs, res_ss, res_rs, stat_ss, stat_rs,
    out_ls, out_ss, out_rs,
):
    o = lax.axis_index("outer")
    n = lax.axis_index("inner")
    c = n % 2
    z = n // 2
    half = z // 8
    zl = z % 8
    quad = z // 4
    zq = z % 4
    gq = zq // 2
    zp = z % 2
    other = 1 - c
    differ = (half + c) % 2
    mate = (o, 2 * z + other)
    zs = z + 1 - 2 * zp
    o1 = o + 1 - 2 * (o % 2)
    o2 = o + 2 - 4 * ((o // 2) % 2)
    o3 = o2 + 1 - 2 * (o2 % 2)
    inputs = (q_in, k_in, v_in)

    def remote(src, dst, ss, rs, device):
        return pltpu.make_async_remote_copy(
            src_ref=src, dst_ref=dst, send_sem=ss, recv_sem=rs, device_id=device, device_id_type=MESH
        )

    def start_either(here, src, dst, ss, rs, device):
        @pl.when(here)
        def _():
            pltpu.make_async_copy(src, dst, rs).start()

        @pl.when(jnp.logical_not(here))
        def _():
            remote(src, dst, ss, rs, device).start()

    def end_either(here, src, dst, ss, rs, device):
        @pl.when(jnp.logical_not(here))
        def _():
            remote(src, dst, ss, rs, device).wait_send()

    quarters = [(quad + shift) % 4 for shift in (2, 1, 3, 0)]

    def load(i, step):
        at = pl.ds(pl.multiple_of(512 * quarters[step], 512), 512)
        return pltpu.make_async_copy(inputs[i].at[:, at], full.at[i, :, at], load_sem.at[step, i])

    for step in range(4):
        for i in range(3):
            load(i, step).start()

    barrier = pltpu.get_barrier_semaphore()

    def greet(d):
        @pl.when(d != n)
        def _():
            pl.semaphore_signal(barrier, inc=1, device_id=(o, d), device_id_type=MESH)

    def greet_line(i, carry):
        greet(16 * c + i)
        return carry

    def greet_quad(i, carry):
        greet(8 * quad + i)
        return carry

    lax.fori_loop(0, 16, greet_line, 0)
    lax.fori_loop(0, 8, greet_quad, 0)
    for line in (o1, o2, o3):
        for cc in range(2):
            pl.semaphore_signal(barrier, inc=1, device_id=(line, 2 * z + cc), device_id_type=MESH)

    own = [
        pltpu.make_async_copy(
            inputs[i].at[:, pl.ds(1024 * c, 1024)], near.at[i, pl.ds(128 * c, 128), :], own_sem.at[i]
        )
        for i in range(3)
    ]
    for copy in own:
        copy.start()

    half128 = halving(128)
    half64 = halving(64)
    half32 = halving(32)

    mine = zl * 2 + c

    def far_route(zz):
        here = zz + 16 * differ == z
        return here, far_s.at[zz], far_r.at[mine], far_ss.at[zz], far_rs.at[mine], (o, 2 * zz + half)

    place = 2 * zp + c

    def level2_routes(k):
        chip = 4 * quad + k
        rows = pl.ds(32 * place, 32)
        heads = pl.ds(4 * k, 4)
        away = (k + 4 - zq) % 4
        return (
            (
                away + (gq + c) % 2 == 0,
                q2_s.at[heads], q2_r.at[:, rows, :], q2_ss.at[k], q2_rs.at[place], (o, 2 * chip + gq),
            ),
            (
                away + (gq + other) % 2 == 0,
                kv2_s.at[heads], kv2_r.at[:, rows, :], kv2_ss.at[k], kv2_rs.at[place], (o, 2 * chip + 1 - gq),
            ),
        )

    for step in range(4):
        part = quarters[step]
        at = pl.ds(pl.multiple_of(512 * part, 512), 512)
        for i in range(3):
            load(i, step).wait()
        one = [nn(half128, full[i, :, at]).astype(BF) for i in range(3)]
        two = [nn(half64, x).astype(BF) for x in one]
        three = [nn(half32, x).astype(BF) for x in two]
        for u in range(4):
            h = part * 4 + u
            cut = slice(u * DIM, (u + 1) * DIM)
            far_s[h] = jnp.concatenate([x[:, cut] for x in three], axis=1)
            q2_s[h] = two[0][:, cut]
            kv2_s[h] = jnp.concatenate([two[1][:, cut], two[2][:, cut]], axis=1)
            kv1_s[h] = jnp.concatenate([one[1][:, cut], one[2][:, cut]], axis=1)
        if step == 0:
            pl.semaphore_wait(barrier, 28 + differ)

        def send_far(u, carry):
            start_either(*far_route(4 * part + u))
            return carry

        lax.fori_loop(0, 4, send_far, 0)
        for route in level2_routes(part):
            start_either(*route)

    near_copies = [
        remote(
            inputs[i].at[:, pl.ds(1024 * other, 1024)], near.at[i, pl.ds(128 * c, 128), :],
            near_ss.at[i], near_rs.at[i], mate,
        )
        for i in range(3)
    ]
    for copy in near_copies:
        copy.start()

    def kv1_copy(q, cc):
        return remote(
            kv1_s.at[pl.ds(HALF * cc + PER * q, PER)],
            kv1_r.at[pl.ds(PER * q, PER), pl.ds(64 * c, 64), :],
            kv1_ss.at[cc, q], kv1_rs.at[c, q], (o, 2 * zs + cc),
        )

    def send_kv1(q, carry):
        for cc in range(2):
            kv1_copy(q, cc).start()
        return carry

    lax.fori_loop(0, CHUNKS, send_kv1, 0)

    for copy in own:
        copy.wait()
    for i in range(3):
        remote(
            inputs[i].at[:, pl.ds(1024 * other, 1024)], near.at[i, pl.ds(128 * other, 128), :],
            near_ss.at[i], near_rs.at[i], mate,
        ).wait_recv()

    def level0(p, carry):
        for u in range(2):
            j = 2 * p + u
            at = pl.ds(pl.multiple_of(j * DIM, DIM), DIM)
            s = nt(near[0, :, at], near[1, :, at])
            peak = jnp.max(s, axis=1, keepdims=True)
            near_o[j] = nn(jnp.exp2((s - peak) * SCALE2).astype(BF), with_ones(near[2, :, at]))
            near_m[j] = jnp.broadcast_to(peak, (256, DIM))
        return carry

    lax.fori_loop(0, HALF // 2, level0, 0)

    def wait_far(s, carry):
        remote(far_s.at[0], far_r.at[s], far_ss.at[0], far_rs.at[s], mate).wait_recv()
        return carry

    lax.fori_loop(0, 16, wait_far, 0)

    for g in range(2):
        kv3 = far_r[pl.ds(8 * g, 8), :, DIM:].reshape(128, 2 * DIM)
        kv4_s[pl.ds(64 * g, 64), :] = nn(half128, kv3).astype(BF)
    kv4_copy = remote(kv4_s, kv4_r, up_ss.at[0], up_rs.at[0], mate)
    kv4_copy.start()
    up = [kv4_copy]
    kv5 = nn(half128, kv4_s[...]).astype(BF)
    kv5_s[...] = kv5
    for cc in range(2):
        copy = remote(kv5_s, kv5_r.at[c], up_ss.at[1 + cc], up_rs.at[1 + c], (o1, 2 * z + cc))
        copy.start()
        up.append(copy)
    kv6_s[...] = nn(half64, kv5).astype(BF)
    slot = 2 * (o % 2) + c
    for k, line in enumerate((o2, o3)):
        for cc in range(2):
            copy = remote(
                kv6_s, kv6_r.at[slot], up_ss.at[3 + 2 * k + cc], up_rs.at[3 + slot], (line, 2 * z + cc)
            )
            copy.start()
            up.append(copy)

    spreads = [halving_spread(128, level) for level in range(1, 4)]
    for g in range(2):
        x = far_r[pl.ds(8 * g, 8), :, :DIM].reshape(128, DIM)
        for level in range(3):
            x = nn(spreads[level], x).astype(BF)
            q_up[level, g] = x

    eye_i, eye_j = grid_of(128, 128)
    eye = eye_i == eye_j

    kv4_copy.wait_recv()
    for cc in range(2):
        remote(kv5_s, kv5_r.at[cc], up_ss.at[1], up_rs.at[1 + cc], mate).wait_recv()
    for s in range(4):
        remote(kv6_s, kv6_r.at[s], up_ss.at[3], up_rs.at[3 + s], mate).wait_recv()

    def results(i):
        device = (o, 2 * (8 * c + i) + half)
        here = 8 * c + i + 16 * differ == z
        return (
            (here, res_s.at[i], res_r.at[zl], res_ss.at[i], res_rs.at[zl], device),
            (here, stat_s.at[i // 4], stat_r.at[zl], stat_ss.at[i], stat_rs.at[zl], device),
        )

    for g in range(2):
        keys = [
            far_r[pl.ds(8 * (1 - g), 8), :, DIM:].reshape(128, 2 * DIM),
            kv4_r[...],
            kv5_r[...].reshape(128, 2 * DIM),
            kv6_r[...].reshape(128, 2 * DIM),
        ]
        queries = [far_r[pl.ds(8 * g, 8), :, :DIM].reshape(128, DIM)] + [q_up[level, g] for level in range(3)]
        scores = [nt(q, kv[:, :DIM]) for q, kv in zip(queries, keys)]
        result, peak, total = attend(scores, [kv[:, DIM:] for kv in keys])
        for i in range(4):
            res_s[4 * g + i] = result[32 * i : 32 * i + 32].astype(BF)
        stat_s[g] = as_rows(eye, peak, total)
        for i in range(4 * g, 4 * g + 4):
            for route in results(i):
                start_either(*route)

    for s in range(4):
        rows = pl.ds(32 * s, 32)
        remote(q2_s.at[pl.ds(0, 4)], q2_r.at[:, rows, :], q2_ss.at[0], q2_rs.at[s], mate).wait_recv()
        remote(kv2_s.at[pl.ds(0, 4)], kv2_r.at[:, rows, :], kv2_ss.at[0], kv2_rs.at[s], mate).wait_recv()
    for u in range(4):
        kv2 = kv2_r[u]
        result, peak, total = attend([nt(q2_r[u], kv2[:, :DIM])], [kv2[:, DIM:]])
        for i in range(2):
            res2_s[i, u] = result[64 * i : 64 * i + 64].astype(BF)
        stat2_s[u] = as_rows(eye, peak, total)

    def level2_results(i):
        k = 2 * c + i
        device = (o, 2 * (4 * quad + k) + gq)
        here = (k + 4 - zq) % 4 + (gq + c) % 2 == 0
        heads = pl.ds(4 * zp, 4)
        return (
            (here, res2_s.at[i], res2_r.at[heads], res2_ss.at[i], res2_rs.at[zp], device),
            (here, stat2_s, stat2_r.at[heads], stat2_ss.at[i], stat2_rs.at[zp], device),
        )

    for i in range(2):
        for route in level2_results(i):
            start_either(*route)

    pairs = halving_spread(256, 1)

    def level1(q, carry):
        for cc in range(2):
            remote(
                kv1_s.at[pl.ds(0, PER)], kv1_r.at[pl.ds(PER * q, PER), pl.ds(64 * cc, 64), :],
                kv1_ss.at[0, q], kv1_rs.at[cc, q], mate,
            ).wait_recv()
        for u in range(PER):
            j = PER * q + u
            at = pl.ds(pl.multiple_of(j * DIM, DIM), DIM)
            x1 = nn(pairs, near[0, :, at]).astype(BF)
            kv1 = kv1_r[j]
            s = nt(x1, kv1[:, :DIM])
            old = near_m[j]
            peak = jnp.maximum(old, jnp.max(s, axis=1, keepdims=True))
            kept = jnp.exp2((old - peak) * SCALE2)
            total = nn(jnp.exp2((s - peak) * SCALE2).astype(BF), with_ones(kv1[:, DIM:]))
            den = kept * near_o[j, :, DIM:] + total[:, DIM:]
            near_o[j, :, :DIM] = (kept * near_o[j, :, :DIM] + total[:, :DIM]) / den
            near_o[j, :, DIM:] = jnp.log(den)
            near_m[j] = peak
        return carry

    lax.fori_loop(0, CHUNKS, level1, 0)

    def repeat_of(level):
        i, j = grid_of(256, 256 >> level)
        return jnp.where((i >> level) == j, 1.0, 0.0).astype(BF)

    def pick_of(level, first):
        i, j = grid_of(256, DIM)
        pick = jnp.where((i >> level) + first == j, 1.0, 0.0).astype(BF)
        return jnp.concatenate([pick, pick, pick], axis=1)

    repeat2, repeat3 = repeat_of(2), repeat_of(3)
    pick2, pick3 = pick_of(2, 64 * zp), pick_of(3, 32 * zq)

    def merge2(p, carry):
        @pl.when(p % 2 == 0)
        def _():
            k = p // 2
            heads = pl.ds(4 * k, 4)
            remote(res2_s.at[0], res2_r.at[heads], res2_ss.at[0], res2_rs.at[k], mate).wait_recv()
            remote(stat2_s, stat2_r.at[heads], stat2_ss.at[0], stat2_rs.at[k], mate).wait_recv()

        for u in range(2):
            j = 2 * p + u
            fine, total, peak = near_o[j, :, :DIM], near_o[j, :, DIM:], near_m[j]
            coarse = nn(repeat2, res2_r[j])
            peak2, total2 = spread_stats(pick2, stat2_r[j])
            top = jnp.maximum(peak, peak2)
            w1 = jnp.exp((peak - top) * SCALE + total)
            w2 = jnp.exp((peak2 - top) * SCALE + total2)
            both = w1 + w2
            near_o[j, :, :DIM] = (w1 * fine + w2 * coarse) / both
            near_o[j, :, DIM:] = jnp.log(both)
            near_m[j] = top
        return carry

    lax.fori_loop(0, HALF // 2, merge2, 0)

    def out_copies(j):
        at = pl.ds(pl.multiple_of((HALF * c + j) * DIM, DIM), DIM)
        return (
            pltpu.make_async_copy(done.at[j, pl.ds(128 * c, 128), :], out.at[:, at], out_ls.at[j]),
            remote(done.at[j, pl.ds(128 * other, 128), :], out.at[:, at], out_ss.at[j], out_rs.at[j], mate),
        )

    for j in range(HALF):
        remote(res_s.at[0], res_r.at[j], res_ss.at[0], res_rs.at[j], mate).wait_recv()
        remote(stat_s.at[0], stat_r.at[j], stat_ss.at[0], stat_rs.at[j], mate).wait_recv()
    columns = nt(pick3, split3(jnp.concatenate([stat_r[j] for j in range(HALF)], axis=0)))
    for j in range(HALF):
        fine, total, peak = near_o[j, :, :DIM], near_o[j, :, DIM:], near_m[j]
        peak3, total3 = columns[:, 2 * j : 2 * j + 1], columns[:, 2 * j + 1 : 2 * j + 2]
        gap = (peak3 - peak) * SCALE + (total3 - total)
        share = 1.0 / (1.0 + jnp.exp(-gap))
        done[j] = (fine + share * (nn(repeat3, res_r[j]) - fine)).astype(BF)
        for copy in out_copies(j):
            copy.start()

    def end_far(k, carry):
        end_either(*far_route(k))
        return carry

    lax.fori_loop(0, 16, end_far, 0)

    def end_level2(i, carry):
        for route in level2_routes(i):
            end_either(*route)
        return carry

    lax.fori_loop(0, 4, end_level2, 0)
    for copy in near_copies:
        copy.wait_send()

    def end_kv1(q, carry):
        for cc in range(2):
            kv1_copy(q, cc).wait_send()
        return carry

    lax.fori_loop(0, CHUNKS, end_kv1, 0)
    for copy in up:
        copy.wait_send()
    for i in range(2):
        for route in level2_results(i):
            end_either(*route)

    def end_results(i, carry):
        for route in results(i):
            end_either(*route)
        return carry

    lax.fori_loop(0, 8, end_results, 0)

    def end_out(j, carry):
        local, far = out_copies(j)
        local.wait()
        far.wait_send()
        at = pl.ds(pl.multiple_of((HALF * other + j) * DIM, DIM), DIM)
        remote(done.at[j, pl.ds(0, 128), :], out.at[:, at], out_ss.at[j], out_rs.at[j], mate).wait_recv()
        return carry

    lax.fori_loop(0, HALF, end_out, 0)


def body(query_states, key_states, value_states):
    dma = pltpu.SemaphoreType.DMA
    vmem = pltpu.VMEM
    return pl.pallas_call(
        kernel,
        out_shape=jax.ShapeDtypeStruct(query_states.shape, BF),
        in_specs=[pl.BlockSpec(memory_space=pltpu.HBM)] * 3,
        out_specs=pl.BlockSpec(memory_space=pl.ANY),
        scratch_shapes=[
            vmem((3, LEAF, HEADS * DIM), BF),
            vmem((3, 2 * LEAF, HALF * DIM), BF),
            vmem((HEADS, 64, 2 * DIM), BF),
            vmem((HALF, 128, 2 * DIM), BF),
            vmem((HEADS, 32, DIM), BF),
            vmem((4, 128, DIM), BF),
            vmem((HEADS, 32, 2 * DIM), BF),
            vmem((4, 128, 2 * DIM), BF),
            vmem((HEADS, 16, 3 * DIM), BF),
            vmem((CHIPS, 16, 3 * DIM), BF),
            vmem((128, 2 * DIM), BF),
            vmem((64, 2 * DIM), BF),
            vmem((32, 2 * DIM), BF),
            vmem((128, 2 * DIM), BF),
            vmem((2, 64, 2 * DIM), BF),
            vmem((4, 32, 2 * DIM), BF),
            vmem((3, 2, 128, DIM), BF),
            vmem((HALF, 256, 2 * DIM), F32),
            vmem((HALF, 256, DIM), F32),
            vmem((2, 4, 64, DIM), BF),
            vmem((4, 2, DIM), F32),
            vmem((8, 64, DIM), BF),
            vmem((8, 2, DIM), F32),
            vmem((8, 32, DIM), BF),
            vmem((2, 2, DIM), F32),
            vmem((8, 32, DIM), BF),
            vmem((8, 2, DIM), F32),
            vmem((HALF, 256, DIM), BF),
            dma((4, 3)), dma((3,)), dma((3,)), dma((3,)), dma((2, CHUNKS)), dma((2, CHUNKS)),
            dma((4,)), dma((4,)), dma((4,)), dma((4,)), dma((16,)), dma((16,)),
            dma((7,)), dma((7,)), dma((2,)), dma((2,)), dma((2,)), dma((2,)),
            dma((8,)), dma((8,)), dma((8,)), dma((8,)),
            dma((8,)), dma((8,)), dma((8,)),
        ],
        compiler_params=pltpu.CompilerParams(
            collective_id=0, has_side_effects=True, vmem_limit_bytes=40 * 1024 * 1024
        ),
        cost_estimate=pl.CostEstimate(flops=600_000_000, bytes_accessed=3_000_000, transcendentals=1_200_000),
        name="tree_attention",
    )(*(pltpu.with_memory_space_constraint(x, pltpu.HBM) for x in (query_states, key_states, value_states)))


def solution(mesh):
    placed = P(("outer", "inner"), None)
    return jax.shard_map(body, mesh=mesh, in_specs=(placed,) * 3, out_specs=placed, check_vma=False)
```

```python
import math

import jax
import jax.numpy as jnp
from jax import lax
from jax.experimental import pallas as pl
from jax.experimental.pallas import tpu as pltpu
from jax.sharding import PartitionSpec as P

HEADS = 16
HALF = HEADS // 2
DIM = 128
LEAF = 128
CHIPS = 16
CHUNKS = 4
PER = HALF // CHUNKS
SCALE = 1.0 / math.sqrt(DIM)
SCALE2 = SCALE * math.log2(math.e)
MESH = pl.DeviceIdType.MESH
BF = jnp.bfloat16
F32 = jnp.float32


def nn(a, b):
    return lax.dot_general(a, b, (((1,), (0,)), ((), ())), preferred_element_type=F32)


def nt(a, b):
    return lax.dot_general(a, b, (((1,), (1,)), ((), ())), preferred_element_type=F32)


def grid_of(rows, columns):
    return (
        lax.broadcasted_iota(jnp.int32, (rows, columns), 0),
        lax.broadcasted_iota(jnp.int32, (rows, columns), 1),
    )


def halving(rows):
    i, j = grid_of(rows // 2, rows)
    return jnp.where((j >> 1) == i, 0.5, 0.0).astype(BF)


def halving_spread(rows, level):
    i, j = grid_of(rows, rows)
    first = (j & ((1 << (level - 1)) - 1)) == 0
    return jnp.where(((i >> level) == (j >> level)) & first, 0.5, 0.0).astype(BF)


def with_ones(values):
    return jnp.concatenate([values, jnp.ones_like(values)], axis=1)


def attend(scores, values):
    peak = jnp.max(scores[0], axis=1, keepdims=True)
    for s in scores[1:]:
        peak = jnp.maximum(peak, jnp.max(s, axis=1, keepdims=True))
    total = None
    for s, v in zip(scores, values):
        w = jnp.exp2((s - peak) * SCALE2).astype(BF)
        part = nn(w, with_ones(v))
        total = part if total is None else total + part
    den = total[:, DIM:]
    return total[:, :DIM] / den, peak, jnp.log(den)


def split3(x):
    high = x.astype(BF)
    rest = x - high.astype(F32)
    mid = rest.astype(BF)
    low = (rest - mid.astype(F32)).astype(BF)
    return jnp.concatenate([high, mid, low], axis=1)


def as_rows(eye, peak, total):
    return jnp.concatenate(
        [
            jnp.sum(jnp.where(eye, peak, 0.0), axis=0, keepdims=True),
            jnp.sum(jnp.where(eye, total, 0.0), axis=0, keepdims=True),
        ],
        axis=0,
    )


def spread_stats(pick3, stats):
    parts = split3(stats)
    both = nt(
        pick3,
        jnp.concatenate(
            [jnp.broadcast_to(parts[0:1], (DIM, 3 * DIM)), jnp.broadcast_to(parts[1:2], (DIM, 3 * DIM))],
            axis=0,
        ),
    )
    return both[:, :DIM], both[:, DIM:]


def kernel(
    q_in, k_in, v_in, out,
    full, near, kv1_s, kv1_r, q2_s, q2_r, kv2_s, kv2_r, far_s, far_r,
    kv4_s, kv5_s, kv6_s, kv4_r, kv5_r, kv6_r, q_up, near_o, near_m,
    res2_s, stat2_s, res2_r, stat2_r, res_s, stat_s, res_r, stat_r, done,
    load_sem, own_sem, near_ss, near_rs, kv1_ss, kv1_rs, q2_ss, q2_rs, kv2_ss, kv2_rs, far_ss, far_rs,
    up_ss, up_rs, res2_ss, res2_rs, stat2_ss, stat2_rs, res_ss, res_rs, stat_ss, stat_rs,
    out_ls, out_ss, out_rs,
):
    o = lax.axis_index("outer")
    n = lax.axis_index("inner")
    c = n % 2
    z = n // 2
    half = z // 8
    zl = z % 8
    quad = z // 4
    zq = z % 4
    gq = zq // 2
    zp = z % 2
    other = 1 - c
    differ = (half + c) % 2
    mate = (o, 2 * z + other)
    zs = z + 1 - 2 * zp
    o1 = o + 1 - 2 * (o % 2)
    o2 = o + 2 - 4 * ((o // 2) % 2)
    o3 = o2 + 1 - 2 * (o2 % 2)
    inputs = (q_in, k_in, v_in)

    def remote(src, dst, ss, rs, device):
        return pltpu.make_async_remote_copy(
            src_ref=src, dst_ref=dst, send_sem=ss, recv_sem=rs, device_id=device, device_id_type=MESH
        )

    def start_either(here, src, dst, ss, rs, device):
        @pl.when(here)
        def _():
            pltpu.make_async_copy(src, dst, rs).start()

        @pl.when(jnp.logical_not(here))
        def _():
            remote(src, dst, ss, rs, device).start()

    def end_either(here, src, dst, ss, rs, device):
        @pl.when(jnp.logical_not(here))
        def _():
            remote(src, dst, ss, rs, device).wait_send()

    quarters = [(quad + shift) % 4 for shift in (2, 1, 3, 0)]

    def load(i, step):
        at = pl.ds(pl.multiple_of(512 * quarters[step], 512), 512)
        return pltpu.make_async_copy(inputs[i].at[:, at], full.at[i, :, at], load_sem.at[step, i])

    barrier = pltpu.get_barrier_semaphore()

    def greet(d):
        @pl.when(d != n)
        def _():
            pl.semaphore_signal(barrier, inc=1, device_id=(o, d), device_id_type=MESH)

    def greet_line(i, carry):
        greet(16 * c + i)
        return carry

    def greet_quad(i, carry):
        greet(8 * quad + i)
        return carry

    lax.fori_loop(0, 16, greet_line, 0)
    lax.fori_loop(0, 8, greet_quad, 0)
    for line in (o1, o2, o3):
        for cc in range(2):
            pl.semaphore_signal(barrier, inc=1, device_id=(line, 2 * z + cc), device_id_type=MESH)

    own = [
        pltpu.make_async_copy(
            inputs[i].at[:, pl.ds(1024 * c, 1024)], near.at[i, pl.ds(128 * c, 128), :], own_sem.at[i]
        )
        for i in range(3)
    ]
    for step in range(4):
        for i in range(3):
            load(i, step).start()

    half128 = halving(128)
    half64 = halving(64)
    half32 = halving(32)

    mine = zl * 2 + c

    def far_route(zz):
        here = zz + 16 * differ == z
        return here, far_s.at[zz], far_r.at[mine], far_ss.at[zz], far_rs.at[mine], (o, 2 * zz + half)

    place = 2 * zp + c

    def level2_routes(k):
        chip = 4 * quad + k
        rows = pl.ds(32 * place, 32)
        heads = pl.ds(4 * k, 4)
        away = (k + 4 - zq) % 4
        return (
            (
                away + (gq + c) % 2 == 0,
                q2_s.at[heads], q2_r.at[:, rows, :], q2_ss.at[k], q2_rs.at[place], (o, 2 * chip + gq),
            ),
            (
                away + (gq + other) % 2 == 0,
                kv2_s.at[heads], kv2_r.at[:, rows, :], kv2_ss.at[k], kv2_rs.at[place], (o, 2 * chip + 1 - gq),
            ),
        )

    for step in range(4):
        part = quarters[step]
        at = pl.ds(pl.multiple_of(512 * part, 512), 512)
        for i in range(3):
            load(i, step).wait()
        one = [nn(half128, full[i, :, at]).astype(BF) for i in range(3)]
        two = [nn(half64, x).astype(BF) for x in one]
        three = [nn(half32, x).astype(BF) for x in two]
        for u in range(4):
            h = part * 4 + u
            cut = slice(u * DIM, (u + 1) * DIM)
            far_s[h] = jnp.concatenate([x[:, cut] for x in three], axis=1)
            q2_s[h] = two[0][:, cut]
            kv2_s[h] = jnp.concatenate([two[1][:, cut], two[2][:, cut]], axis=1)
            kv1_s[h] = jnp.concatenate([one[1][:, cut], one[2][:, cut]], axis=1)
        if step == 0:
            pl.semaphore_wait(barrier, 28 + differ)

        def send_far(u, carry):
            start_either(*far_route(4 * part + u))
            return carry

        lax.fori_loop(0, 4, send_far, 0)
        for route in level2_routes(part):
            start_either(*route)

    near_copies = [
        remote(
            inputs[i].at[:, pl.ds(1024 * other, 1024)], near.at[i, pl.ds(128 * c, 128), :],
            near_ss.at[i], near_rs.at[i], mate,
        )
        for i in range(3)
    ]
    for copy in own:
        copy.start()

    for copy in near_copies:
        copy.start()

    def kv1_copy(q, cc):
        return remote(
            kv1_s.at[pl.ds(HALF * cc + PER * q, PER)],
            kv1_r.at[pl.ds(PER * q, PER), pl.ds(64 * c, 64), :],
            kv1_ss.at[cc, q], kv1_rs.at[c, q], (o, 2 * zs + cc),
        )

    def send_kv1(q, carry):
        for cc in range(2):
            kv1_copy(q, cc).start()
        return carry

    lax.fori_loop(0, CHUNKS, send_kv1, 0)

    for copy in own:
        copy.wait()
    for i in range(3):
        remote(
            inputs[i].at[:, pl.ds(1024 * other, 1024)], near.at[i, pl.ds(128 * other, 128), :],
            near_ss.at[i], near_rs.at[i], mate,
        ).wait_recv()

    def level0(p, carry):
        for u in range(2):
            j = 2 * p + u
            at = pl.ds(pl.multiple_of(j * DIM, DIM), DIM)
            s = nt(near[0, :, at], near[1, :, at])
            peak = jnp.max(s, axis=1, keepdims=True)
            near_o[j] = nn(jnp.exp2((s - peak) * SCALE2).astype(BF), with_ones(near[2, :, at]))
            near_m[j] = jnp.broadcast_to(peak, (256, DIM))
        return carry

    lax.fori_loop(0, HALF // 2, level0, 0)

    def wait_far(s, carry):
        remote(far_s.at[0], far_r.at[s], far_ss.at[0], far_rs.at[s], mate).wait_recv()
        return carry

    lax.fori_loop(0, 16, wait_far, 0)

    for g in range(2):
        kv3 = far_r[pl.ds(8 * g, 8), :, DIM:].reshape(128, 2 * DIM)
        kv4_s[pl.ds(64 * g, 64), :] = nn(half128, kv3).astype(BF)
    kv4_copy = remote(kv4_s, kv4_r, up_ss.at[0], up_rs.at[0], mate)
    kv4_copy.start()
    up = [kv4_copy]
    kv5 = nn(half128, kv4_s[...]).astype(BF)
    kv5_s[...] = kv5
    for cc in range(2):
        copy = remote(kv5_s, kv5_r.at[c], up_ss.at[1 + cc], up_rs.at[1 + c], (o1, 2 * z + cc))
        copy.start()
        up.append(copy)
    kv6_s[...] = nn(half64, kv5).astype(BF)
    slot = 2 * (o % 2) + c
    for k, line in enumerate((o2, o3)):
        for cc in range(2):
            copy = remote(
                kv6_s, kv6_r.at[slot], up_ss.at[3 + 2 * k + cc], up_rs.at[3 + slot], (line, 2 * z + cc)
            )
            copy.start()
            up.append(copy)

    spreads = [halving_spread(128, level) for level in range(1, 4)]
    for g in range(2):
        x = far_r[pl.ds(8 * g, 8), :, :DIM].reshape(128, DIM)
        for level in range(3):
            x = nn(spreads[level], x).astype(BF)
            q_up[level, g] = x

    eye_i, eye_j = grid_of(128, 128)
    eye = eye_i == eye_j

    kv4_copy.wait_recv()
    for cc in range(2):
        remote(kv5_s, kv5_r.at[cc], up_ss.at[1], up_rs.at[1 + cc], mate).wait_recv()
    for s in range(4):
        remote(kv6_s, kv6_r.at[s], up_ss.at[3], up_rs.at[3 + s], mate).wait_recv()

    def results(i):
        device = (o, 2 * (8 * c + i) + half)
        here = 8 * c + i + 16 * differ == z
        return (
            (here, res_s.at[i], res_r.at[zl], res_ss.at[i], res_rs.at[zl], device),
            (here, stat_s.at[i // 4], stat_r.at[zl], stat_ss.at[i], stat_rs.at[zl], device),
        )

    for g in range(2):
        keys = [
            far_r[pl.ds(8 * (1 - g), 8), :, DIM:].reshape(128, 2 * DIM),
            kv4_r[...],
            kv5_r[...].reshape(128, 2 * DIM),
            kv6_r[...].reshape(128, 2 * DIM),
        ]
        queries = [far_r[pl.ds(8 * g, 8), :, :DIM].reshape(128, DIM)] + [q_up[level, g] for level in range(3)]
        scores = [nt(q, kv[:, :DIM]) for q, kv in zip(queries, keys)]
        result, peak, total = attend(scores, [kv[:, DIM:] for kv in keys])
        for i in range(4):
            res_s[4 * g + i] = result[32 * i : 32 * i + 32].astype(BF)
        stat_s[g] = as_rows(eye, peak, total)
        for i in range(4 * g, 4 * g + 4):
            for route in results(i):
                start_either(*route)

    for s in range(4):
        rows = pl.ds(32 * s, 32)
        remote(q2_s.at[pl.ds(0, 4)], q2_r.at[:, rows, :], q2_ss.at[0], q2_rs.at[s], mate).wait_recv()
        remote(kv2_s.at[pl.ds(0, 4)], kv2_r.at[:, rows, :], kv2_ss.at[0], kv2_rs.at[s], mate).wait_recv()
    for u in range(4):
        kv2 = kv2_r[u]
        result, peak, total = attend([nt(q2_r[u], kv2[:, :DIM])], [kv2[:, DIM:]])
        for i in range(2):
            res2_s[i, u] = result[64 * i : 64 * i + 64].astype(BF)
        stat2_s[u] = as_rows(eye, peak, total)

    def level2_results(i):
        k = 2 * c + i
        device = (o, 2 * (4 * quad + k) + gq)
        here = (k + 4 - zq) % 4 + (gq + c) % 2 == 0
        heads = pl.ds(4 * zp, 4)
        return (
            (here, res2_s.at[i], res2_r.at[heads], res2_ss.at[i], res2_rs.at[zp], device),
            (here, stat2_s, stat2_r.at[heads], stat2_ss.at[i], stat2_rs.at[zp], device),
        )

    for i in range(2):
        for route in level2_results(i):
            start_either(*route)

    pairs = halving_spread(256, 1)

    def level1(q, carry):
        for cc in range(2):
            remote(
                kv1_s.at[pl.ds(0, PER)], kv1_r.at[pl.ds(PER * q, PER), pl.ds(64 * cc, 64), :],
                kv1_ss.at[0, q], kv1_rs.at[cc, q], mate,
            ).wait_recv()
        for u in range(PER):
            j = PER * q + u
            at = pl.ds(pl.multiple_of(j * DIM, DIM), DIM)
            x1 = nn(pairs, near[0, :, at]).astype(BF)
            kv1 = kv1_r[j]
            s = nt(x1, kv1[:, :DIM])
            old = near_m[j]
            peak = jnp.maximum(old, jnp.max(s, axis=1, keepdims=True))
            kept = jnp.exp2((old - peak) * SCALE2)
            total = nn(jnp.exp2((s - peak) * SCALE2).astype(BF), with_ones(kv1[:, DIM:]))
            den = kept * near_o[j, :, DIM:] + total[:, DIM:]
            near_o[j, :, :DIM] = (kept * near_o[j, :, :DIM] + total[:, :DIM]) / den
            near_o[j, :, DIM:] = jnp.log(den)
            near_m[j] = peak
        return carry

    lax.fori_loop(0, CHUNKS, level1, 0)

    def repeat_of(level):
        i, j = grid_of(256, 256 >> level)
        return jnp.where((i >> level) == j, 1.0, 0.0).astype(BF)

    def pick_of(level, first):
        i, j = grid_of(256, DIM)
        pick = jnp.where((i >> level) + first == j, 1.0, 0.0).astype(BF)
        return jnp.concatenate([pick, pick, pick], axis=1)

    repeat2, repeat3 = repeat_of(2), repeat_of(3)
    pick2, pick3 = pick_of(2, 64 * zp), pick_of(3, 32 * zq)

    for k in range(2):
        heads = pl.ds(4 * k, 4)
        remote(res2_s.at[0], res2_r.at[heads], res2_ss.at[0], res2_rs.at[k], mate).wait_recv()
        remote(stat2_s, stat2_r.at[heads], stat2_ss.at[0], stat2_rs.at[k], mate).wait_recv()
    columns = nt(pick2, split3(jnp.concatenate([stat2_r[j] for j in range(HALF)], axis=0)))
    for j in range(HALF):
        fine, total, peak = near_o[j, :, :DIM], near_o[j, :, DIM:], near_m[j]
        peak2, total2 = columns[:, 2 * j : 2 * j + 1], columns[:, 2 * j + 1 : 2 * j + 2]
        top = jnp.maximum(peak, peak2)
        w1 = jnp.exp((peak - top) * SCALE + total)
        w2 = jnp.exp((peak2 - top) * SCALE + total2)
        both = w1 + w2
        near_o[j, :, :DIM] = (w1 * fine + w2 * nn(repeat2, res2_r[j])) / both
        near_o[j, :, DIM:] = jnp.log(both)
        near_m[j] = top

    def out_copies(j):
        at = pl.ds(pl.multiple_of((HALF * c + j) * DIM, DIM), DIM)
        return (
            pltpu.make_async_copy(done.at[j, pl.ds(128 * c, 128), :], out.at[:, at], out_ls.at[j]),
            remote(done.at[j, pl.ds(128 * other, 128), :], out.at[:, at], out_ss.at[j], out_rs.at[j], mate),
        )

    for j in range(HALF):
        remote(res_s.at[0], res_r.at[j], res_ss.at[0], res_rs.at[j], mate).wait_recv()
        remote(stat_s.at[0], stat_r.at[j], stat_ss.at[0], stat_rs.at[j], mate).wait_recv()
    columns = nt(pick3, split3(jnp.concatenate([stat_r[j] for j in range(HALF)], axis=0)))
    for j in range(HALF):
        fine, total, peak = near_o[j, :, :DIM], near_o[j, :, DIM:], near_m[j]
        peak3, total3 = columns[:, 2 * j : 2 * j + 1], columns[:, 2 * j + 1 : 2 * j + 2]
        gap = (peak3 - peak) * SCALE + (total3 - total)
        share = 1.0 / (1.0 + jnp.exp(-gap))
        done[j] = (fine + share * (nn(repeat3, res_r[j]) - fine)).astype(BF)
        for copy in reversed(out_copies(j)):
            copy.start()

    def end_far(k, carry):
        end_either(*far_route(k))
        return carry

    lax.fori_loop(0, 16, end_far, 0)

    def end_level2(i, carry):
        for route in level2_routes(i):
            end_either(*route)
        return carry

    lax.fori_loop(0, 4, end_level2, 0)
    for copy in near_copies:
        copy.wait_send()

    def end_kv1(q, carry):
        for cc in range(2):
            kv1_copy(q, cc).wait_send()
        return carry

    lax.fori_loop(0, CHUNKS, end_kv1, 0)
    for copy in up:
        copy.wait_send()
    for i in range(2):
        for route in level2_results(i):
            end_either(*route)

    def end_results(i, carry):
        for route in results(i):
            end_either(*route)
        return carry

    lax.fori_loop(0, 8, end_results, 0)

    def end_out(j, carry):
        local, far = out_copies(j)
        local.wait()
        far.wait_send()
        at = pl.ds(pl.multiple_of((HALF * other + j) * DIM, DIM), DIM)
        remote(done.at[j, pl.ds(0, 128), :], out.at[:, at], out_ss.at[j], out_rs.at[j], mate).wait_recv()
        return carry

    lax.fori_loop(0, HALF, end_out, 0)


def body(query_states, key_states, value_states):
    dma = pltpu.SemaphoreType.DMA
    vmem = pltpu.VMEM
    return pl.pallas_call(
        kernel,
        out_shape=jax.ShapeDtypeStruct(query_states.shape, BF),
        in_specs=[pl.BlockSpec(memory_space=pltpu.HBM)] * 3,
        out_specs=pl.BlockSpec(memory_space=pl.ANY),
        scratch_shapes=[
            vmem((3, LEAF, HEADS * DIM), BF),
            vmem((3, 2 * LEAF, HALF * DIM), BF),
            vmem((HEADS, 64, 2 * DIM), BF),
            vmem((HALF, 128, 2 * DIM), BF),
            vmem((HEADS, 32, DIM), BF),
            vmem((4, 128, DIM), BF),
            vmem((HEADS, 32, 2 * DIM), BF),
            vmem((4, 128, 2 * DIM), BF),
            vmem((HEADS, 16, 3 * DIM), BF),
            vmem((CHIPS, 16, 3 * DIM), BF),
            vmem((128, 2 * DIM), BF),
            vmem((64, 2 * DIM), BF),
            vmem((32, 2 * DIM), BF),
            vmem((128, 2 * DIM), BF),
            vmem((2, 64, 2 * DIM), BF),
            vmem((4, 32, 2 * DIM), BF),
            vmem((3, 2, 128, DIM), BF),
            vmem((HALF, 256, 2 * DIM), F32),
            vmem((HALF, 256, DIM), F32),
            vmem((2, 4, 64, DIM), BF),
            vmem((4, 2, DIM), F32),
            vmem((8, 64, DIM), BF),
            vmem((8, 2, DIM), F32),
            vmem((8, 32, DIM), BF),
            vmem((2, 2, DIM), F32),
            vmem((8, 32, DIM), BF),
            vmem((8, 2, DIM), F32),
            vmem((HALF, 256, DIM), BF),
            dma((4, 3)), dma((3,)), dma((3,)), dma((3,)), dma((2, CHUNKS)), dma((2, CHUNKS)),
            dma((4,)), dma((4,)), dma((4,)), dma((4,)), dma((16,)), dma((16,)),
            dma((7,)), dma((7,)), dma((2,)), dma((2,)), dma((2,)), dma((2,)),
            dma((8,)), dma((8,)), dma((8,)), dma((8,)),
            dma((8,)), dma((8,)), dma((8,)),
        ],
        compiler_params=pltpu.CompilerParams(
            collective_id=0, has_side_effects=True, vmem_limit_bytes=40 * 1024 * 1024
        ),
        cost_estimate=pl.CostEstimate(flops=600_000_000, bytes_accessed=3_000_000, transcendentals=1_200_000),
        name="tree_attention",
    )(*(pltpu.with_memory_space_constraint(x, pltpu.HBM) for x in (query_states, key_states, value_states)))


def solution(mesh):
    placed = P(("outer", "inner"), None)
    return jax.shard_map(body, mesh=mesh, in_specs=(placed,) * 3, out_specs=placed, check_vma=False)
```
